32 devices in a mesh: hours: 4 (over y, core), surf: 8 (over z, x).
Axes of the slice: x: 2, y: 2, z: 4, core: 2. Of those that a mesh axis runs over, the one named last changes fastest.
Arguments:
- sky_radiance: bfloat16 [256, 2304], P('hours'), parts along dimension 0, may hold values from 0.049804688 to 20
- surf_coeff: bfloat16 [128, 8, 128, 128], P('surf'), may hold values from 0 to 0.001953125
- surf_patch: int32 [128, 8], P('surf'), may hold values from 0 to 17
- surf_count: int32 [128], P('surf'), may hold values from 1 to 8, as said below
- sens_coeff: bfloat16 [192, 8, 128, 128], P('surf'), may hold values from 0 to 0.001953125
- sens_patch: int32 [192, 8], P('surf'), may hold values from 0 to 17
- sens_count: int32 [192], P('surf'), may hold values from 1 to 8, as said below
- albedo: float32 [16384], P('surf'), may hold values from 0.08 to 0.8
- view_tile: bfloat16 [128, 8, 128, 128], P('surf')
- view_peer: int32 [128, 8], P('surf'), may hold values from 0 to 7, as said below
- wanted: int32 [8, 8], P('surf'), may hold values from 0 to 15
- sens_surf: int32 [2, 24576], P(None, 'surf'), may hold values from 0 to 16383, as said below
- sens_weight: float32 [2, 24576], P(None, 'surf'), may hold values from 0.2 to 1
Outputs:
- surf_irradiance: float32 [256, 16384], P('hours', 'surf'), parts along dimension 0
- sens_irradiance: float32 [256, 24576], P('hours', 'surf'), parts along dimension 0
The draws below stay inside these ranges and needn't reach their ends.
There are 4 independent parts, one for each index of `hours`. The reference program is written for one: setup_inputs(seed, part) draws one part's arguments, and reference() takes and returns one part's arrays. A program takes and returns all parts, laid end to end along the dimension named above; an argument that names none is the same for every part. Nothing has to cross between parts.
Inputs may be any that keep to these rules, and one draw needn't show every extreme that they name: `surf_count`: at least 1 and at most 8; some block has 8. `sens_count`: at least 1 and at most 8; some block has 8. `view_peer`: the 128 entries of one device name every device at least once. `sens_surf`: each sensor's surfaces lie on the device that holds the sensor.
All inputs are finite; a program needn't handle non-finite values.
Results may differ from the reference program's by a relative error of at most 0.0003.
Values may be sent and summed in bfloat16 or wider, within the bound.
A program may use at most 128 MiB of HBM per device.

```python
import math
import jax
import jax.numpy as jnp
from jax import lax

P_SIZE = 2304
TILE = 128
H = 64
KS = 8
KR = 8
KF = 8
BLK_DEV = 16
RB_DEV = 24
PT = 18
SB = 128
S_TOTAL = 16384
RBT = 192
R_TOTAL = 24576
N_SURF = 8


def tile_totals(key, block_count, most_tiles):
    per_device = block_count // N_SURF
    device_caps = jax.random.randint(jax.random.fold_in(key, 11), (N_SURF,), 2, most_tiles + 1)
    device_cap = jnp.repeat(device_caps, per_device, total_repeat_length=block_count)
    raw_values = jax.random.randint(jax.random.fold_in(key, 12), (block_count,), 0, 1 << 20)
    drawn_vals = 1 + raw_values % device_cap
    chosen = jax.random.randint(jax.random.fold_in(key, 13), (), 0, block_count)
    return jnp.where(jnp.arange(block_count) == chosen, most_tiles, drawn_vals).astype(jnp.int32)


def draw_surf_count(key, part):
    return tile_totals(key, BLK_DEV * N_SURF, KS)


def draw_sens_count(key, part):
    return tile_totals(key, RB_DEV * N_SURF, KR)


def draw_view_tile(key, part):
    block_count = BLK_DEV * N_SURF
    full_shape = (block_count, KF, TILE, TILE)
    shifts = jax.random.randint(jax.random.fold_in(key, 41), (block_count, KF, 1, 1), 0, TILE)
    seen_index = jnp.arange(TILE, dtype=jnp.int32).reshape(1, 1, TILE, 1)
    seeing_index = jnp.arange(TILE, dtype=jnp.int32).reshape(1, 1, 1, TILE)
    on_peak = (seeing_index + shifts) % TILE == seen_index
    peak_value = jax.random.uniform(jax.random.fold_in(key, 42), (block_count, KF, 1, TILE), jnp.float32, 0.5, 1.5)
    background = jax.random.uniform(jax.random.fold_in(key, 43), full_shape, jnp.float32) * (0.8 / TILE)
    overall = 0.9 / (1.4 * KF)
    values = overall * jnp.where(on_peak, peak_value, background)
    return values.astype(jnp.bfloat16)


def draw_view_peer(key, part):
    device_keys = jax.random.split(jax.random.fold_in(key, 21), N_SURF)

    def one_device(sub_key):
        return jax.random.permutation(sub_key, BLK_DEV * KF) % N_SURF
    return jax.vmap(one_device)(device_keys).reshape(N_SURF * BLK_DEV, KF).astype(jnp.int32)


def draw_sens_surf(key, part):
    sensor_total = RB_DEV * TILE * N_SURF
    device_ids = jnp.arange(sensor_total, dtype=jnp.int32) // (RB_DEV * TILE)
    picks = jax.random.randint(jax.random.fold_in(key, 31), (2, sensor_total), 0, BLK_DEV * TILE)
    return (device_ids[None, :] * (BLK_DEV * TILE) + picks).astype(jnp.int32)


def with_ends(array, stream_key, low, high):
    dims = array.shape
    index_at = [jax.random.randint(jax.random.fold_in(stream_key, axis), (), 0, dims[axis]) for axis in range(len(dims))]
    array = array.at[tuple(index_at)].set(low)
    longest = dims.index(max(dims))
    index_at[longest] = (index_at[longest] + 1) % dims[longest]
    return array.at[tuple(index_at)].set(high)


def levels(key, shape, pieces, low, top_value):
    level = 1.0
    for axis_at, parts in pieces:
        heights = jax.random.uniform(jax.random.fold_in(jax.random.fold_in(key, 6), axis_at), (parts,), jnp.float32, low / len(pieces), top_value / len(pieces))
        level = level * jnp.repeat(jnp.exp(heights), shape[axis_at] // parts).reshape((-1,) + (1,) * (len(shape) - 1 - axis_at))
    return level


def setup_inputs(seed: int = 0, part: int = 0) -> dict:
    splits = jax.random.split(jax.random.key(seed), 14)
    part_keys = jax.random.split(jax.random.fold_in(splits[13], part), 14)
    sky_radiance = jnp.clip(jnp.exp(jax.random.uniform(part_keys[0], (H, P_SIZE), jnp.float32, math.log(0.049804688), math.log(20.0))), 0.049804688, 20.0).astype(jnp.bfloat16)
    surf_coeff = jnp.clip(0.001953125 * jax.random.uniform(splits[1], (SB, KS, TILE, TILE), jnp.float32) ** levels(splits[1], (SB, KS, TILE, TILE), ((0, 8),), -0.2, 0.2), 0.0, 0.001953125).astype(jnp.bfloat16)
    surf_patch = with_ends(jax.random.randint(splits[2], (SB, KS), 0, PT), jax.random.fold_in(splits[2], 1), 0, PT - 1).astype(jnp.int32)
    surf_count = draw_surf_count(jax.random.fold_in(splits[13], 71), part)
    sens_coeff = jnp.clip(0.001953125 * jax.random.uniform(splits[4], (RBT, KR, TILE, TILE), jnp.float32) ** levels(splits[4], (RBT, KR, TILE, TILE), ((0, 8),), -0.2, 0.2), 0.0, 0.001953125).astype(jnp.bfloat16)
    sens_patch = with_ends(jax.random.randint(splits[5], (RBT, KR), 0, PT), jax.random.fold_in(splits[5], 1), 0, PT - 1).astype(jnp.int32)
    sens_count = draw_sens_count(jax.random.fold_in(splits[13], 71), part)
    albedo = jnp.clip(jnp.exp(math.log(0.8) - 2.3025851 * jax.random.uniform(splits[7], (S_TOTAL,), jnp.float32) ** levels(splits[7], (S_TOTAL,), ((0, 8),), -0.2, 0.2)), 0.08, 0.8)
    view_tile = draw_view_tile(jax.random.fold_in(splits[13], 71), part)
    view_peer = draw_view_peer(jax.random.fold_in(splits[13], 71), part)
    wanted = with_ends(jax.random.randint(splits[10], (N_SURF, N_SURF), 0, BLK_DEV), jax.random.fold_in(splits[10], 1), 0, BLK_DEV - 1).astype(jnp.int32)
    sens_surf = draw_sens_surf(jax.random.fold_in(splits[13], 71), part)
    sens_weight = jnp.clip(0.2 + 0.8 * jax.random.uniform(splits[12], (2, R_TOTAL), jnp.float32) ** levels(splits[12], (2, R_TOTAL), ((1, 8),), -0.2, 0.2), 0.2, 1.0)
    return dict(sky_radiance=sky_radiance, surf_coeff=surf_coeff, surf_patch=surf_patch, surf_count=surf_count, sens_coeff=sens_coeff, sens_patch=sens_patch, sens_count=sens_count, albedo=albedo, view_tile=view_tile, view_peer=view_peer, wanted=wanted, sens_surf=sens_surf, sens_weight=sens_weight)


def sky_blocks(sky_radiance, coeff, patches, tile_counts):
    hour_rows = sky_radiance.shape[0]
    block_rows, per_block, tile_edge, _ = coeff.shape
    sky_tiles = sky_radiance.astype(jnp.float32).reshape(hour_rows, -1, tile_edge)
    slot_order = jnp.arange(per_block, dtype=jnp.int32)

    def one_block(packed):
        coef_tile, patch_index, tile_total = packed
        picked = jnp.take(sky_tiles, patch_index, axis=1)
        kept_mask = (slot_order < tile_total).astype(jnp.float32)
        return jnp.einsum('hkp,kps->hs', picked * kept_mask[None, :, None], coef_tile.astype(jnp.float32))

    summed = lax.map(one_block, (coeff, patches, tile_counts))
    return jnp.transpose(summed, (1, 0, 2)).reshape(hour_rows, block_rows * tile_edge)


def bounce(energy, albedo, view_tile, view_peer, wanted):
    hour_rows = energy.shape[0]
    block_rows, per_block, tile_edge, _ = view_tile.shape
    rounded = lax.optimization_barrier((energy * albedo[None, :]).astype(jnp.bfloat16))
    radiosity = rounded.astype(jnp.float32)
    per_device = block_rows // N_SURF
    owner_dev = jnp.arange(block_rows, dtype=jnp.int32) // per_device
    target = view_peer * per_device + wanted[owner_dev[:, None], view_peer]
    whole_grid = radiosity.reshape(hour_rows, block_rows, tile_edge)

    def one_block(packed):
        view_block, target_row = packed
        column_rows = jnp.take(whole_grid, target_row, axis=1)
        return jnp.einsum('hkc,kcr->hr', column_rows, view_block.astype(jnp.float32))

    summed = lax.map(one_block, (view_tile, target.astype(jnp.int32)))
    return jnp.transpose(summed, (1, 0, 2)).reshape(hour_rows, block_rows * tile_edge)


def reference(sky_radiance, surf_coeff, surf_patch, surf_count, sens_coeff, sens_patch, sens_count, albedo, view_tile, view_peer, wanted, sens_surf, sens_weight):
    direct = sky_blocks(sky_radiance, surf_coeff, surf_patch, surf_count)
    first_pass = direct + bounce(direct, albedo, view_tile, view_peer, wanted)
    reflected = bounce(first_pass, albedo, view_tile, view_peer, wanted)
    surf_irradiance = direct + reflected
    sens_direct = sky_blocks(sky_radiance, sens_coeff, sens_patch, sens_count)
    near_first = jnp.take(reflected, sens_surf[0], axis=1)
    near_second = jnp.take(reflected, sens_surf[1], axis=1)
    sens_irradiance = sens_direct + sens_weight[0][None, :] * near_first + sens_weight[1][None, :] * near_second
    return surf_irradiance, sens_irradiance
```

```python
import functools

import jax
import jax.numpy as jnp
from jax import lax
from jax.experimental import pallas as pl
from jax.experimental.pallas import tpu as pltpu
from jax.sharding import PartitionSpec as P

F32 = jnp.float32
BF16 = jnp.bfloat16
F8 = jnp.float8_e4m3fn

TOP = 256.0
STEP = 32.0


def wide_dot(table, picks, weights):
    lhs = jnp.concatenate([table[i] for i in picks], axis=1)
    return jnp.dot(lhs, weights, preferred_element_type=F32)


def farthest_first(n):
    if n > 8 or n & (n - 1):
        return None
    return [*range(n - 1, 0, -2), *range(n - 2, 0, -2)]


def kernel(
    n,
    sky_hbm,
    surf_hbm,
    surf_patch_hbm,
    surf_count_hbm,
    sens_hbm,
    sens_patch_hbm,
    sens_count_hbm,
    albedo_hbm,
    view_hbm,
    view_peer_hbm,
    wanted_hbm,
    sens_surf_hbm,
    sens_weight_hbm,
    surf_out,
    sens_out,
    pieces,
    onehot,
    gain,
    sky,
    surf_patch,
    surf_count,
    sens_patch,
    sens_count,
    albedo,
    view_peer,
    sens_surf,
    sens_weight,
    sky_tab,
    surf_w,
    sens_w,
    view_w,
    direct,
    rad,
    refl,
    send_a,
    send_b,
    slots_a,
    slots_b,
    want_own,
    want_v,
    want_s,
    small_sem,
    load_sem,
    want_sem,
    send_sem,
    recv_sem,
):
    hours, patch_width = sky.shape
    blocks, depth, tile = view_w.shape
    sens_blocks = sens_w.shape[0]
    per = depth // tile
    patches = patch_width // tile
    me = lax.axis_index("surf")
    far = farthest_first(n)

    def out_to(step):
        if far is None:
            return lax.rem(me + step, n)
        to = me
        for bit in (1, 2, 4):
            if step & bit:
                to = to + bit * (1 - 2 * lax.rem(me // bit, 2))
        return to

    def in_from(step):
        return lax.rem(me + n - step, n) if far is None else out_to(step)

    barrier = pltpu.get_barrier_semaphore()

    def loop(low, high, body, group):
        count = high - low
        group = next(g for g in range(min(group, count), 0, -1) if count % g == 0)

        def go(i, carry):
            for u in range(group):
                body(low + i * group + u)
            return carry

        lax.fori_loop(0, count // group, go, 0)

    def each(turn, body):
        if far is None:
            loop(1, n, lambda step: body(turn(step)), 7)
        else:
            for step in range(1, n):
                body(turn(step))

    def each_far(body):
        if far is None:
            each(out_to, body)
        else:
            for step in far:
                body(out_to(step))

    def greet(peer):
        pl.semaphore_signal(
            barrier, inc=1, device_id={"surf": peer}, device_id_type=pl.DeviceIdType.MESH
        )

    each(out_to, greet)

    surf_parts = load_parts(blocks)
    sens_parts = load_parts(sens_blocks)

    def part(hbm, vmem, parts, i, first):
        size = vmem.shape[0] // parts
        span = pl.ds(i * size, size)
        return pltpu.make_async_copy(hbm.at[span], vmem.at[span], load_sem.at[first + i])

    surf_loads = [part(surf_hbm, surf_w, surf_parts, i, 0) for i in range(surf_parts)]
    view_load = part(view_hbm, view_w, 1, 0, surf_parts)
    sens_loads = [
        part(sens_hbm, sens_w, sens_parts, i, surf_parts + 1) for i in range(sens_parts)
    ]
    small = (
        (wanted_hbm.at[0], want_own),
        (wanted_hbm.at[0], want_v.at[me]),
        (sky_hbm, sky),
        (surf_patch_hbm, surf_patch),
        (surf_count_hbm, surf_count),
        (albedo_hbm, albedo),
        (view_peer_hbm, view_peer),
        (sens_patch_hbm, sens_patch),
        (sens_count_hbm, sens_count),
        (sens_surf_hbm, sens_surf),
        (sens_weight_hbm, sens_weight),
    )
    small_loads = [
        pltpu.make_async_copy(src, dst, small_sem.at[i]) for i, (src, dst) in enumerate(small)
    ]
    early, late = small_loads[:6], small_loads[6:]
    for copy in (*early, *surf_loads, *late, *sens_loads[:2], view_load, *sens_loads[2:]):
        copy.start()

    def remote(src, dst, kind, to, mine):
        return pltpu.make_async_remote_copy(
            src_ref=src,
            dst_ref=dst.at[mine],
            send_sem=send_sem.at[kind, to],
            recv_sem=recv_sem.at[kind, mine],
            device_id={"surf": to},
            device_id_type=pl.DeviceIdType.MESH,
        )

    early[0].wait()
    pl.semaphore_wait(barrier, n - 1)
    each_far(lambda e: remote(want_own, want_v, 0, e, me).start())

    early[2].wait()
    for j in range(patches):
        sky_tab[j] = sky[:, j * tile : (j + 1) * tile]
    sky_tab[patches] = jnp.zeros((hours, tile), BF16)

    def live(patch, count, k, b):
        return jnp.where(k < count[b], patch[k, b], patches)

    def direct_block(b):
        picks = [live(surf_patch, surf_count, k, b) for k in range(per)]
        value = wide_dot(sky_tab, picks, surf_w[b])
        direct[b] = value
        rad[b] = (value * albedo[b]).astype(BF16)

    def sens_block(b):
        picks = [live(sens_patch, sens_count, k, b) for k in range(per)]
        cols = pl.ds(pl.multiple_of(b * tile, tile), tile)
        sens_out[:, cols] = wide_dot(sky_tab, picks, sens_w[b])

    for copy in (early[1], *early[3:]):
        copy.wait()
    for i, copy in enumerate(surf_loads):
        copy.wait()
        size = blocks // surf_parts
        loop(i * size, (i + 1) * size, direct_block, 4)

    for copy in late:
        copy.wait()

    each(in_from, lambda e: remote(want_own, want_v, 0, me, e).wait_recv())
    to_smem = pltpu.make_async_copy(want_v, want_s, want_sem.at[0])
    to_smem.start()
    to_smem.wait()

    def asked(e):
        return want_s[e, 0, me]

    def first_send(e):
        send_a[e] = rad[asked(e)]
        remote(send_a.at[e], slots_a, 1, e, me).start()

    each(in_from, first_send)
    slots_a[me] = rad[asked(me)]

    half = sens_parts // 2
    rows = lax.broadcasted_iota(jnp.int32, (tile, 2 * tile), 0).astype(jnp.int16)
    ones = jnp.ones((tile, 2 * tile), BF16)
    zeros = jnp.zeros((tile, 2 * tile), BF16)

    def onehot_block(r):
        cols = pl.ds(pl.multiple_of(r * tile, tile), tile)
        index = sens_surf[:, cols] - me * (blocks * tile)
        index = jnp.concatenate([index[0:1], index[1:2]], axis=1)
        index = jnp.broadcast_to(index, (tile, 2 * tile)).astype(jnp.int16)
        for s in range(blocks):
            hit = rows == index - jnp.int16(s * tile)
            onehot[r, s * tile : (s + 1) * tile, :] = jnp.where(hit, ones, zeros).astype(F8)

    def sens_part(i):
        sens_loads[i].wait()
        size = sens_blocks // sens_parts
        loop(i * size, (i + 1) * size, sens_block, 6)
        loop(i * size, (i + 1) * size, onehot_block, 1)

    for i in range(half):
        sens_part(i)

    view_load.wait()
    each(in_from, lambda e: remote(send_a.at[e], slots_a, 1, me, e).wait_recv())

    def bounced(slots, b):
        picks = [view_peer[k, b] for k in range(per)]
        return wide_dot(slots, picks, view_w[b])

    def second_value(b):
        value = direct[b] + bounced(slots_a, b)
        return (value * albedo[b]).astype(BF16)

    def second_send(e):
        send_b[e] = second_value(asked(e))
        remote(send_b.at[e], slots_b, 2, e, me).start()

    each_far(second_send)
    slots_b[me] = second_value(asked(me))

    for i in range(half, sens_parts):
        sens_part(i)

    each(in_from, lambda e: remote(send_b.at[e], slots_b, 2, me, e).wait_recv())

    group = 8 if blocks % 8 == 0 else 1

    def last_blocks(i, most):
        for u in range(group):
            b = i * group + u
            value = bounced(slots_b, b)
            cols = pl.ds(pl.multiple_of(b * tile, tile), tile)
            refl[:, cols] = value
            surf_out[:, cols] = direct[b] + value
            most = jnp.maximum(most, jnp.abs(value))
        return most

    most = lax.fori_loop(0, blocks // group, last_blocks, jnp.full((hours, tile), 1e-30, F32))
    most = jnp.max(jnp.max(most, axis=0, keepdims=True), axis=1, keepdims=True)
    gain[...] = sens_weight[...] * (most * (1 / TOP))
    rest = refl[...] * (TOP / most)
    for i in range(3):
        piece = rest.astype(F8)
        pieces[i * hours : (i + 1) * hours, :] = piece
        rest = (rest - piece.astype(F32)) * STEP

    each(out_to, lambda e: remote(want_own, want_v, 0, e, me).wait_send())
    each(out_to, lambda e: remote(send_a.at[e], slots_a, 1, e, me).wait_send())
    each(out_to, lambda e: remote(send_b.at[e], slots_b, 2, e, me).wait_send())


def load_parts(blocks):
    return 4 if blocks % 4 == 0 else 1


def local(
    sky_radiance,
    surf_coeff,
    surf_patch,
    surf_count,
    sens_coeff,
    sens_patch,
    sens_count,
    albedo,
    view_tile,
    view_peer,
    wanted,
    sens_surf,
    sens_weight,
):
    n = lax.axis_size("surf")
    hours, patch_width = sky_radiance.shape
    blocks, per, tile, _ = view_tile.shape
    sens_blocks = sens_coeff.shape[0]
    depth = per * tile
    patches = patch_width // tile

    hbm = pl.BlockSpec(memory_space=pltpu.HBM)
    vmem = pl.BlockSpec(memory_space=pltpu.VMEM)
    loads = load_parts(blocks) + 1 + load_parts(sens_blocks)
    made = pl.pallas_call(
        functools.partial(kernel, n),
        out_shape=(
            pltpu.VMEM((hours, blocks * tile), F32),
            pltpu.VMEM((hours, sens_blocks * tile), F32),
            pltpu.VMEM((3 * hours, blocks * tile), F8),
            pltpu.VMEM((sens_blocks, blocks * tile, 2 * tile), F8),
            pltpu.VMEM(sens_weight.shape, F32),
        ),
        in_specs=[hbm] * 13,
        out_specs=(vmem,) * 5,
        scratch_shapes=[
            pltpu.VMEM((hours, patch_width), BF16),
            pltpu.SMEM((per, blocks), jnp.int32),
            pltpu.SMEM((blocks,), jnp.int32),
            pltpu.SMEM((per, sens_blocks), jnp.int32),
            pltpu.SMEM((sens_blocks,), jnp.int32),
            pltpu.VMEM((blocks, 1, tile), F32),
            pltpu.SMEM((per, blocks), jnp.int32),
            pltpu.VMEM(sens_surf.shape, jnp.int32),
            pltpu.VMEM(sens_weight.shape, F32),
            pltpu.VMEM((patches + 1, hours, tile), BF16),
            pltpu.VMEM((blocks, depth, tile), BF16),
            pltpu.VMEM((sens_blocks, depth, tile), BF16),
            pltpu.VMEM((blocks, depth, tile), BF16),
            pltpu.VMEM((blocks, hours, tile), F32),
            pltpu.VMEM((blocks, hours, tile), BF16),
            pltpu.VMEM((hours, blocks * tile), F32),
            pltpu.VMEM((n, hours, tile), BF16),
            pltpu.VMEM((n, hours, tile), BF16),
            pltpu.VMEM((n, hours, tile), BF16),
            pltpu.VMEM((n, hours, tile), BF16),
            pltpu.VMEM((1, n), jnp.int32),
            pltpu.VMEM((n, 1, n), jnp.int32),
            pltpu.SMEM((n, 1, n), jnp.int32),
            pltpu.SemaphoreType.DMA((11,)),
            pltpu.SemaphoreType.DMA((loads,)),
            pltpu.SemaphoreType.DMA((2,)),
            pltpu.SemaphoreType.DMA((3, n)),
            pltpu.SemaphoreType.DMA((3, n)),
        ],
        compiler_params=pltpu.CompilerParams(
            collective_id=0, has_side_effects=True, vmem_limit_bytes=24 * 2**20
        ),
    )(
        *(
            pltpu.with_memory_space_constraint(a, pltpu.HBM)
            for a in (
                sky_radiance,
                surf_coeff.reshape(blocks, depth, tile),
                surf_patch.T,
                surf_count,
                sens_coeff.reshape(sens_blocks, depth, tile),
                sens_patch.T,
                sens_count,
                albedo.reshape(blocks, 1, tile),
                view_tile.reshape(blocks, depth, tile),
                view_peer.T,
                wanted.reshape(1, 1, n),
                sens_surf,
                sens_weight,
            )
        )
    )
    return sensors(*made)


def near(parts, surf, sens, pieces, onehot, gain, surf_hbm, sens_hbm, out, sem):
    hours = surf.shape[0]
    sens_blocks, _, tile = onehot.shape
    tile //= 2
    stores = [pltpu.make_async_copy(surf, surf_hbm, sem.at[0])]
    stores[0].start()
    size = sens_blocks // parts
    for i in range(parts):
        for r in range(i * size, (i + 1) * size):
            cols = pl.ds(r * tile, tile)
            found = jnp.dot(pieces[...], onehot[r], preferred_element_type=F32)
            found = found[:hours] + (1 / STEP) * (
                found[hours : 2 * hours] + (1 / STEP) * found[2 * hours :]
            )
            weight = gain[:, cols]
            out[:, cols] = (
                sens[:, cols]
                + weight[0:1] * found[:, :tile]
                + weight[1:2] * found[:, tile:]
            )
        cols = pl.ds(i * size * tile, size * tile)
        copy = pltpu.make_async_copy(out.at[:, cols], sens_hbm.at[:, cols], sem.at[1 + i])
        copy.start()
        stores.append(copy)
    for copy in stores:
        copy.wait()


def sensors(*arrays):
    surf, sens = arrays[:2]
    parts = load_parts(arrays[3].shape[0])
    hbm = pl.BlockSpec(memory_space=pltpu.HBM)
    vmem = pl.BlockSpec(memory_space=pltpu.VMEM)
    return pl.pallas_call(
        functools.partial(near, parts),
        out_shape=(
            jax.ShapeDtypeStruct(surf.shape, F32),
            jax.ShapeDtypeStruct(sens.shape, F32),
        ),
        in_specs=[vmem] * 5,
        out_specs=(hbm, hbm),
        scratch_shapes=[pltpu.VMEM(sens.shape, F32), pltpu.SemaphoreType.DMA((1 + parts,))],
        compiler_params=pltpu.CompilerParams(vmem_limit_bytes=8 * 2**20),
    )(*(pltpu.with_memory_space_constraint(a, pltpu.VMEM) for a in arrays))


def solution(mesh):
    in_specs = (
        P("hours", None),
        P("surf", None, None, None),
        P("surf", None),
        P("surf"),
        P("surf", None, None, None),
        P("surf", None),
        P("surf"),
        P("surf"),
        P("surf", None, None, None),
        P("surf", None),
        P("surf", None),
        P(None, "surf"),
        P(None, "surf"),
    )
    out_specs = (P("hours", "surf"), P("hours", "surf"))
    return jax.shard_map(local, mesh=mesh, in_specs=in_specs, out_specs=out_specs, check_vma=False)
```

```python
import functools

import jax
import jax.numpy as jnp
from jax import lax
from jax.experimental import pallas as pl
from jax.experimental.pallas import tpu as pltpu
from jax.sharding import PartitionSpec as P

F32 = jnp.float32
BF16 = jnp.bfloat16
F8 = jnp.float8_e4m3fn

TOP = 256.0
STEP = 32.0


def wide_dot(table, picks, weights):
    lhs = jnp.concatenate([table[i] for i in picks], axis=1)
    return jnp.dot(lhs, weights, preferred_element_type=F32)


def farthest_first(n):
    if n > 8 or n & (n - 1):
        return None
    return [*range(n - 1, 0, -2), *range(n - 2, 0, -2)]


def kernel(
    n,
    sky_hbm,
    surf_hbm,
    surf_patch_hbm,
    surf_count_hbm,
    sens_hbm,
    sens_patch_hbm,
    sens_count_hbm,
    albedo_hbm,
    view_hbm,
    view_peer_hbm,
    wanted_hbm,
    sens_surf_hbm,
    sens_weight_hbm,
    surf_out,
    sens_out,
    pieces,
    onehot,
    gain,
    sky,
    surf_patch,
    surf_count,
    sens_patch,
    sens_count,
    albedo,
    view_peer,
    sens_surf,
    sens_weight,
    sky_tab,
    surf_w,
    sens_w,
    view_w,
    direct,
    rad,
    refl,
    send_a,
    send_b,
    slots_a,
    slots_b,
    want_own,
    want_rows,
    want_v,
    want_s,
    small_sem,
    load_sem,
    want_sem,
    send_sem,
    recv_sem,
):
    hours, patch_width = sky.shape
    blocks, depth, tile = view_w.shape
    sens_blocks = sens_w.shape[0]
    per = depth // tile
    patches = patch_width // tile
    me = lax.axis_index("surf")
    far = farthest_first(n)

    def out_to(step):
        if far is None:
            return lax.rem(me + step, n)
        to = me
        for bit in (1, 2, 4):
            if step & bit:
                to = to + bit * (1 - 2 * lax.rem(me // bit, 2))
        return to

    def in_from(step):
        return lax.rem(me + n - step, n) if far is None else out_to(step)

    barrier = pltpu.get_barrier_semaphore()

    def loop(low, high, body, group):
        count = high - low
        group = next(g for g in range(min(group, count), 0, -1) if count % g == 0)

        def go(i, carry):
            for u in range(group):
                body(low + i * group + u)
            return carry

        lax.fori_loop(0, count // group, go, 0)

    def each(turn, body):
        if far is None:
            loop(1, n, lambda step: body(turn(step)), 7)
        else:
            for step in range(1, n):
                body(turn(step))

    def each_far(body):
        if far is None:
            each(out_to, body)
        else:
            for step in far:
                body(out_to(step))

    def greet(peer):
        pl.semaphore_signal(
            barrier, inc=1, device_id={"surf": peer}, device_id_type=pl.DeviceIdType.MESH
        )

    each(out_to, greet)

    surf_parts = load_parts(blocks)
    sens_parts = load_parts(sens_blocks)

    def part(hbm, vmem, parts, i, first):
        size = vmem.shape[0] // parts
        span = pl.ds(i * size, size)
        return pltpu.make_async_copy(hbm.at[span], vmem.at[span], load_sem.at[first + i])

    surf_loads = [part(surf_hbm, surf_w, surf_parts, i, 0) for i in range(surf_parts)]
    view_load = part(view_hbm, view_w, 1, 0, surf_parts)
    sens_loads = [
        part(sens_hbm, sens_w, sens_parts, i, surf_parts + 1) for i in range(sens_parts)
    ]
    small = (
        (wanted_hbm.at[0], want_own),
        (sky_hbm, sky),
        (surf_patch_hbm, surf_patch),
        (surf_count_hbm, surf_count),
        (albedo_hbm, albedo),
        (view_peer_hbm, view_peer),
        (sens_patch_hbm, sens_patch),
        (sens_count_hbm, sens_count),
        (sens_surf_hbm, sens_surf),
        (sens_weight_hbm, sens_weight),
    )
    small_loads = [
        pltpu.make_async_copy(src, dst, small_sem.at[i]) for i, (src, dst) in enumerate(small)
    ]
    early, late = small_loads[:5], small_loads[5:]
    for copy in (*early, *surf_loads, *late, *sens_loads[:2], view_load, *sens_loads[2:]):
        copy.start()

    def remote(src, dst, kind, to, mine):
        return pltpu.make_async_remote_copy(
            src_ref=src,
            dst_ref=dst.at[mine],
            send_sem=send_sem.at[kind, to],
            recv_sem=recv_sem.at[kind, mine],
            device_id={"surf": to},
            device_id_type=pl.DeviceIdType.MESH,
        )

    early[0].wait()
    for e in range(n):
        want_rows[e] = jnp.full(want_rows.shape[1:], want_own[0, e], jnp.int32)
    want_v[me] = want_rows[me]
    pl.semaphore_wait(barrier, n - 1)
    each_far(lambda e: remote(want_rows.at[e], want_v, 0, e, me).start())

    early[1].wait()
    for j in range(patches):
        sky_tab[j] = sky[:, j * tile : (j + 1) * tile]
    sky_tab[patches] = jnp.zeros((hours, tile), BF16)

    def live(patch, count, k, b):
        return jnp.where(k < count[b], patch[k, b], patches)

    def direct_block(b):
        picks = [live(surf_patch, surf_count, k, b) for k in range(per)]
        value = wide_dot(sky_tab, picks, surf_w[b])
        direct[b] = value
        rad[b] = (value * albedo[b]).astype(BF16)

    def sens_block(b):
        picks = [live(sens_patch, sens_count, k, b) for k in range(per)]
        cols = pl.ds(pl.multiple_of(b * tile, tile), tile)
        sens_out[:, cols] = wide_dot(sky_tab, picks, sens_w[b])

    for copy in early[2:]:
        copy.wait()
    for i, copy in enumerate(surf_loads):
        copy.wait()
        size = blocks // surf_parts
        loop(i * size, (i + 1) * size, direct_block, 4)

    for copy in late:
        copy.wait()

    def first_send(e):
        remote(want_rows.at[e], want_v, 0, me, e).wait_recv()
        send_a[e] = rad[jnp.max(want_v[e])]
        remote(send_a.at[e], slots_a, 1, e, me).start()

    each(in_from, first_send)
    slots_a[me] = rad[jnp.max(want_v[me])]
    to_smem = pltpu.make_async_copy(want_v, want_s, want_sem.at[0])
    to_smem.start()

    half = sens_parts // 2
    rows = lax.broadcasted_iota(jnp.int32, (tile, 2 * tile), 0).astype(jnp.int16)
    ones = jnp.ones((tile, 2 * tile), BF16)
    zeros = jnp.zeros((tile, 2 * tile), BF16)

    def onehot_block(r):
        cols = pl.ds(pl.multiple_of(r * tile, tile), tile)
        index = sens_surf[:, cols] - me * (blocks * tile)
        index = jnp.concatenate([index[0:1], index[1:2]], axis=1)
        index = jnp.broadcast_to(index, (tile, 2 * tile)).astype(jnp.int16)
        for s in range(blocks):
            hit = rows == index - jnp.int16(s * tile)
            onehot[r, s * tile : (s + 1) * tile, :] = jnp.where(hit, ones, zeros).astype(F8)

    def sens_part(i):
        sens_loads[i].wait()
        size = sens_blocks // sens_parts
        loop(i * size, (i + 1) * size, sens_block, 6)
        loop(i * size, (i + 1) * size, onehot_block, 1)

    for i in range(half):
        sens_part(i)

    view_load.wait()
    to_smem.wait()
    each(in_from, lambda e: remote(send_a.at[e], slots_a, 1, me, e).wait_recv())

    def bounced(slots, b):
        picks = [view_peer[k, b] for k in range(per)]
        return wide_dot(slots, picks, view_w[b])

    def asked(e):
        return want_s[e, 0, 0]

    def second_value(b):
        value = direct[b] + bounced(slots_a, b)
        return (value * albedo[b]).astype(BF16)

    def second_send(e):
        send_b[e] = second_value(asked(e))
        remote(send_b.at[e], slots_b, 2, e, me).start()

    each_far(second_send)
    slots_b[me] = second_value(asked(me))

    for i in range(half, sens_parts):
        sens_part(i)

    each(in_from, lambda e: remote(send_b.at[e], slots_b, 2, me, e).wait_recv())

    group = next(g for g in (16, 8, 4, 2, 1) if blocks % g == 0)

    def last_blocks(i, most):
        for u in range(group):
            b = i * group + u
            value = bounced(slots_b, b)
            cols = pl.ds(pl.multiple_of(b * tile, tile), tile)
            refl[:, cols] = value
            surf_out[:, cols] = direct[b] + value
            most = jnp.maximum(most, jnp.abs(value))
        return most

    most = lax.fori_loop(0, blocks // group, last_blocks, jnp.full((hours, tile), 1e-30, F32))
    most = jnp.max(jnp.max(most, axis=0, keepdims=True), axis=1, keepdims=True)
    gain[...] = sens_weight[...] * (most * (1 / TOP))
    rest = refl[...] * (TOP / most)
    for i in range(3):
        piece = rest.astype(F8)
        pieces[i * hours : (i + 1) * hours, :] = piece
        rest = (rest - piece.astype(F32)) * STEP

    each(out_to, lambda e: remote(want_rows.at[e], want_v, 0, e, me).wait_send())
    each(out_to, lambda e: remote(send_a.at[e], slots_a, 1, e, me).wait_send())
    each(out_to, lambda e: remote(send_b.at[e], slots_b, 2, e, me).wait_send())


def load_parts(blocks):
    return 4 if blocks % 4 == 0 else 1


def local(
    sky_radiance,
    surf_coeff,
    surf_patch,
    surf_count,
    sens_coeff,
    sens_patch,
    sens_count,
    albedo,
    view_tile,
    view_peer,
    wanted,
    sens_surf,
    sens_weight,
):
    n = lax.axis_size("surf")
    hours, patch_width = sky_radiance.shape
    blocks, per, tile, _ = view_tile.shape
    sens_blocks = sens_coeff.shape[0]
    depth = per * tile
    patches = patch_width // tile

    hbm = pl.BlockSpec(memory_space=pltpu.HBM)
    vmem = pl.BlockSpec(memory_space=pltpu.VMEM)
    loads = load_parts(blocks) + 1 + load_parts(sens_blocks)
    made = pl.pallas_call(
        functools.partial(kernel, n),
        out_shape=(
            pltpu.VMEM((hours, blocks * tile), F32),
            pltpu.VMEM((hours, sens_blocks * tile), F32),
            pltpu.VMEM((3 * hours, blocks * tile), F8),
            pltpu.VMEM((sens_blocks, blocks * tile, 2 * tile), F8),
            pltpu.VMEM(sens_weight.shape, F32),
        ),
        in_specs=[hbm] * 13,
        out_specs=(vmem,) * 5,
        scratch_shapes=[
            pltpu.VMEM((hours, patch_width), BF16),
            pltpu.SMEM((per, blocks), jnp.int32),
            pltpu.SMEM((blocks,), jnp.int32),
            pltpu.SMEM((per, sens_blocks), jnp.int32),
            pltpu.SMEM((sens_blocks,), jnp.int32),
            pltpu.VMEM((blocks, 1, tile), F32),
            pltpu.SMEM((per, blocks), jnp.int32),
            pltpu.VMEM(sens_surf.shape, jnp.int32),
            pltpu.VMEM(sens_weight.shape, F32),
            pltpu.VMEM((patches + 1, hours, tile), BF16),
            pltpu.VMEM((blocks, depth, tile), BF16),
            pltpu.VMEM((sens_blocks, depth, tile), BF16),
            pltpu.VMEM((blocks, depth, tile), BF16),
            pltpu.VMEM((blocks, hours, tile), F32),
            pltpu.VMEM((blocks, hours, tile), BF16),
            pltpu.VMEM((hours, blocks * tile), F32),
            pltpu.VMEM((n, hours, tile), BF16),
            pltpu.VMEM((n, hours, tile), BF16),
            pltpu.VMEM((n, hours, tile), BF16),
            pltpu.VMEM((n, hours, tile), BF16),
            pltpu.SMEM((1, n), jnp.int32),
            pltpu.VMEM((n, 1, tile), jnp.int32),
            pltpu.VMEM((n, 1, tile), jnp.int32),
            pltpu.SMEM((n, 1, tile), jnp.int32),
            pltpu.SemaphoreType.DMA((10,)),
            pltpu.SemaphoreType.DMA((loads,)),
            pltpu.SemaphoreType.DMA((2,)),
            pltpu.SemaphoreType.DMA((3, n)),
            pltpu.SemaphoreType.DMA((3, n)),
        ],
        compiler_params=pltpu.CompilerParams(
            collective_id=0, has_side_effects=True, vmem_limit_bytes=24 * 2**20
        ),
    )(
        *(
            pltpu.with_memory_space_constraint(a, pltpu.HBM)
            for a in (
                sky_radiance,
                surf_coeff.reshape(blocks, depth, tile),
                surf_patch.T,
                surf_count,
                sens_coeff.reshape(sens_blocks, depth, tile),
                sens_patch.T,
                sens_count,
                albedo.reshape(blocks, 1, tile),
                view_tile.reshape(blocks, depth, tile),
                view_peer.T,
                wanted.reshape(1, 1, n),
                sens_surf,
                sens_weight,
            )
        )
    )
    return sensors(*made)


def near(parts, surf, sens, pieces, onehot, gain, surf_hbm, sens_hbm, out, sem):
    hours = surf.shape[0]
    tile = onehot.shape[2] // 2
    stores = [pltpu.make_async_copy(surf, surf_hbm, sem.at[0])]
    stores[0].start()
    low = 0
    for i, high in enumerate(parts):
        for r in range(low, high):
            cols = pl.ds(r * tile, tile)
            found = jnp.dot(pieces[...], onehot[r], preferred_element_type=F32)
            found = found[:hours] + (1 / STEP) * (
                found[hours : 2 * hours] + (1 / STEP) * found[2 * hours :]
            )
            weight = gain[:, cols]
            out[:, cols] = (
                sens[:, cols]
                + weight[0:1] * found[:, :tile]
                + weight[1:2] * found[:, tile:]
            )
        cols = pl.ds(low * tile, (high - low) * tile)
        copy = pltpu.make_async_copy(out.at[:, cols], sens_hbm.at[:, cols], sem.at[1 + i])
        copy.start()
        stores.append(copy)
        low = high
    for copy in stores:
        copy.wait()


def sensors(*arrays):
    surf, sens = arrays[:2]
    count = arrays[3].shape[0]
    parts = [*range(6, count - 5, 6), count - 2, count] if count > 6 else [count]
    hbm = pl.BlockSpec(memory_space=pltpu.HBM)
    vmem = pl.BlockSpec(memory_space=pltpu.VMEM)
    return pl.pallas_call(
        functools.partial(near, parts),
        out_shape=(
            jax.ShapeDtypeStruct(surf.shape, F32),
            jax.ShapeDtypeStruct(sens.shape, F32),
        ),
        in_specs=[vmem] * 5,
        out_specs=(hbm, hbm),
        scratch_shapes=[pltpu.VMEM(sens.shape, F32), pltpu.SemaphoreType.DMA((1 + len(parts),))],
        compiler_params=pltpu.CompilerParams(vmem_limit_bytes=8 * 2**20),
    )(*(pltpu.with_memory_space_constraint(a, pltpu.VMEM) for a in arrays))


def solution(mesh):
    in_specs = (
        P("hours", None),
        P("surf", None, None, None),
        P("surf", None),
        P("surf"),
        P("surf", None, None, None),
        P("surf", None),
        P("surf"),
        P("surf"),
        P("surf", None, None, None),
        P("surf", None),
        P("surf", None),
        P(None, "surf"),
        P(None, "surf"),
    )
    out_specs = (P("hours", "surf"), P("hours", "surf"))
    return jax.shard_map(local, mesh=mesh, in_specs=in_specs, out_specs=out_specs, check_vma=False)
```

```python
import functools

import jax
import jax.numpy as jnp
from jax import lax
from jax.experimental import pallas as pl
from jax.experimental.pallas import tpu as pltpu
from jax.sharding import PartitionSpec as P

F32 = jnp.float32
BF16 = jnp.bfloat16
F8 = jnp.float8_e4m3fn

TOP = 256.0
STEP = 32.0


def wide_dot(table, picks, weights):
    lhs = jnp.concatenate([table[i] for i in picks], axis=1)
    return jnp.dot(lhs, weights, preferred_element_type=F32)


def farthest_first(n):
    if n > 8 or n & (n - 1):
        return None
    return [*range(n - 1, 0, -2), *range(n - 2, 0, -2)]


def kernel(
    n,
    sky_hbm,
    surf_hbm,
    surf_patch_hbm,
    surf_count_hbm,
    sens_hbm,
    sens_patch_hbm,
    sens_count_hbm,
    albedo_hbm,
    view_hbm,
    view_peer_hbm,
    wanted_hbm,
    sens_surf_hbm,
    sens_weight_hbm,
    surf_out,
    sens_out,
    refl,
    most,
    onehot,
    place,
    weight,
    sky,
    surf_patch,
    surf_count,
    sens_patch,
    sens_count,
    albedo,
    view_peer,
    sens_surf,
    sky_tab,
    surf_w,
    sens_w,
    view_w,
    direct,
    rad,
    send_a,
    send_b,
    slots_a,
    slots_b,
    want_own,
    want_rows,
    want_v,
    want_s,
    small_sem,
    load_sem,
    want_sem,
    send_sem,
    recv_sem,
):
    hours, patch_width = sky.shape
    blocks, depth, tile = view_w.shape
    sens_blocks = sens_w.shape[0]
    per = depth // tile
    patches = patch_width // tile
    me = lax.axis_index("surf")
    far = farthest_first(n)

    def out_to(step):
        if far is None:
            return lax.rem(me + step, n)
        to = me
        for bit in (1, 2, 4):
            if step & bit:
                to = to + bit * (1 - 2 * lax.rem(me // bit, 2))
        return to

    def in_from(step):
        return lax.rem(me + n - step, n) if far is None else out_to(step)

    barrier = pltpu.get_barrier_semaphore()

    def loop(low, high, body, group):
        count = high - low
        group = next(g for g in range(min(group, count), 0, -1) if count % g == 0)

        def go(i, carry):
            for u in range(group):
                body(low + i * group + u)
            return carry

        lax.fori_loop(0, count // group, go, 0)

    def each(turn, body):
        if far is None:
            loop(1, n, lambda step: body(turn(step)), 7)
        else:
            for step in range(1, n):
                body(turn(step))

    def each_far(body):
        if far is None:
            each(out_to, body)
        else:
            for step in far:
                body(out_to(step))

    def greet(peer):
        pl.semaphore_signal(
            barrier, inc=1, device_id={"surf": peer}, device_id_type=pl.DeviceIdType.MESH
        )

    each_far(greet)

    surf_parts = load_parts(blocks)
    sens_parts = load_parts(sens_blocks)

    def part(hbm, vmem, parts, i, first):
        size = vmem.shape[0] // parts
        span = pl.ds(i * size, size)
        return pltpu.make_async_copy(hbm.at[span], vmem.at[span], load_sem.at[first + i])

    surf_loads = [part(surf_hbm, surf_w, surf_parts, i, 0) for i in range(surf_parts)]
    view_load = part(view_hbm, view_w, 1, 0, surf_parts)
    sens_loads = [
        part(sens_hbm, sens_w, sens_parts, i, surf_parts + 1) for i in range(sens_parts)
    ]
    small = (
        (wanted_hbm.at[0], want_own),
        (sky_hbm, sky),
        (surf_patch_hbm, surf_patch),
        (surf_count_hbm, surf_count),
        (albedo_hbm, albedo),
        (view_peer_hbm, view_peer),
        (sens_patch_hbm, sens_patch),
        (sens_count_hbm, sens_count),
        (sens_surf_hbm, sens_surf),
        (sens_weight_hbm, weight),
    )
    small_loads = [
        pltpu.make_async_copy(src, dst, small_sem.at[i]) for i, (src, dst) in enumerate(small)
    ]
    early, late = small_loads[:5], small_loads[5:]
    for copy in (*early, *surf_loads, *late):
        copy.start()

    def remote(src, dst, kind, to, mine):
        return pltpu.make_async_remote_copy(
            src_ref=src,
            dst_ref=dst.at[mine],
            send_sem=send_sem.at[kind, to],
            recv_sem=recv_sem.at[kind, mine],
            device_id={"surf": to},
            device_id_type=pl.DeviceIdType.MESH,
        )

    early[0].wait()
    for e in range(n):
        want_rows[e] = jnp.full(want_rows.shape[1:], want_own[0, e], jnp.int32)
    want_v[me] = want_rows[me]
    pl.semaphore_wait(barrier, n - 1)
    each_far(lambda e: remote(want_rows.at[e], want_v, 0, e, me).start())

    early[1].wait()
    for j in range(patches):
        sky_tab[j] = sky[:, j * tile : (j + 1) * tile]
    sky_tab[patches] = jnp.zeros((hours, tile), BF16)

    def live(patch, count, k, b):
        return jnp.where(k < count[b], patch[k, b], patches)

    def direct_block(b):
        picks = [live(surf_patch, surf_count, k, b) for k in range(per)]
        value = wide_dot(sky_tab, picks, surf_w[b])
        direct[b] = value
        rad[b] = (value * albedo[b]).astype(BF16)

    def sens_block(b):
        picks = [live(sens_patch, sens_count, k, b) for k in range(per)]
        cols = pl.ds(pl.multiple_of(b * tile, tile), tile)
        sens_out[:, cols] = wide_dot(sky_tab, picks, sens_w[b])

    for copy in early[2:]:
        copy.wait()
    for i, copy in enumerate(surf_loads):
        copy.wait()
        size = blocks // surf_parts
        loop(i * size, (i + 1) * size, direct_block, 4)

    for copy in late:
        copy.wait()
    for copy in (*sens_loads[:2], view_load, *sens_loads[2:]):
        copy.start()
    place[...] = sens_surf[...] - me * (blocks * tile)

    def first_send(e):
        remote(want_rows.at[e], want_v, 0, me, e).wait_recv()
        send_a[e] = rad[jnp.max(want_v[e])]
        remote(send_a.at[e], slots_a, 1, e, me).start()

    each(in_from, first_send)
    slots_a[me] = rad[jnp.max(want_v[me])]
    to_smem = pltpu.make_async_copy(want_v, want_s, want_sem.at[0])
    to_smem.start()

    half = sens_parts // 2
    rows = lax.broadcasted_iota(jnp.int32, (tile, 2 * tile), 0).astype(jnp.int16)
    ones = jnp.ones((tile, 2 * tile), BF16)
    zeros = jnp.zeros((tile, 2 * tile), BF16)

    def onehot_block(r):
        cols = pl.ds(pl.multiple_of(r * tile, tile), tile)
        index = place[:, cols]
        index = jnp.concatenate([index[0:1], index[1:2]], axis=1)
        index = jnp.broadcast_to(index, (tile, 2 * tile)).astype(jnp.int16)
        for s in range(blocks):
            hit = rows == index - jnp.int16(s * tile)
            onehot[r, s * tile : (s + 1) * tile, :] = jnp.where(hit, ones, zeros).astype(F8)

    def sens_part(i):
        sens_loads[i].wait()
        size = sens_blocks // sens_parts
        loop(i * size, (i + 1) * size, sens_block, 6)
        loop(i * size, (i + 1) * size, onehot_block, 1)

    for i in range(half):
        sens_part(i)

    view_load.wait()
    to_smem.wait()
    each(in_from, lambda e: remote(send_a.at[e], slots_a, 1, me, e).wait_recv())

    def bounced(slots, b):
        picks = [view_peer[k, b] for k in range(per)]
        return wide_dot(slots, picks, view_w[b])

    def asked(e):
        return want_s[e, 0, 0]

    def second_value(b):
        value = direct[b] + bounced(slots_a, b)
        return (value * albedo[b]).astype(BF16)

    def second_send(e):
        send_b[e] = second_value(asked(e))
        remote(send_b.at[e], slots_b, 2, e, me).start()

    each_far(second_send)
    slots_b[me] = second_value(asked(me))

    for i in range(half, sens_parts):
        sens_part(i)

    each(in_from, lambda e: remote(send_b.at[e], slots_b, 2, me, e).wait_recv())

    group = next(g for g in (16, 8, 4, 2, 1) if blocks % g == 0)

    def last_blocks(i, top):
        for u in range(group):
            b = i * group + u
            value = bounced(slots_b, b)
            cols = pl.ds(pl.multiple_of(b * tile, tile), tile)
            refl[:, cols] = value
            surf_out[:, cols] = direct[b] + value
            top = jnp.maximum(top, jnp.abs(value))
        return top

    most[...] = lax.fori_loop(0, blocks // group, last_blocks, jnp.full((hours, tile), 1e-30, F32))

    each(out_to, lambda e: remote(want_rows.at[e], want_v, 0, e, me).wait_send())
    each(out_to, lambda e: remote(send_a.at[e], slots_a, 1, e, me).wait_send())
    each(out_to, lambda e: remote(send_b.at[e], slots_b, 2, e, me).wait_send())


def load_parts(blocks):
    return 4 if blocks % 4 == 0 else 1


def local(
    sky_radiance,
    surf_coeff,
    surf_patch,
    surf_count,
    sens_coeff,
    sens_patch,
    sens_count,
    albedo,
    view_tile,
    view_peer,
    wanted,
    sens_surf,
    sens_weight,
):
    n = lax.axis_size("surf")
    hours, patch_width = sky_radiance.shape
    blocks, per, tile, _ = view_tile.shape
    sens_blocks = sens_coeff.shape[0]
    depth = per * tile
    patches = patch_width // tile

    hbm = pl.BlockSpec(memory_space=pltpu.HBM)
    vmem = pl.BlockSpec(memory_space=pltpu.VMEM)
    loads = load_parts(blocks) + 1 + load_parts(sens_blocks)
    made = pl.pallas_call(
        functools.partial(kernel, n),
        out_shape=(
            pltpu.VMEM((hours, blocks * tile), F32),
            pltpu.VMEM((hours, sens_blocks * tile), F32),
            pltpu.VMEM((hours, blocks * tile), F32),
            pltpu.VMEM((hours, tile), F32),
            pltpu.VMEM((sens_blocks, blocks * tile, 2 * tile), F8),
            pltpu.VMEM(sens_surf.shape, jnp.int32),
            pltpu.VMEM(sens_weight.shape, F32),
        ),
        in_specs=[hbm] * 13,
        out_specs=(vmem,) * 7,
        scratch_shapes=[
            pltpu.VMEM((hours, patch_width), BF16),
            pltpu.SMEM((per, blocks), jnp.int32),
            pltpu.SMEM((blocks,), jnp.int32),
            pltpu.SMEM((per, sens_blocks), jnp.int32),
            pltpu.SMEM((sens_blocks,), jnp.int32),
            pltpu.VMEM((blocks, 1, tile), F32),
            pltpu.SMEM((per, blocks), jnp.int32),
            pltpu.VMEM(sens_surf.shape, jnp.int32),
            pltpu.VMEM((patches + 1, hours, tile), BF16),
            pltpu.VMEM((blocks, depth, tile), BF16),
            pltpu.VMEM((sens_blocks, depth, tile), BF16),
            pltpu.VMEM((blocks, depth, tile), BF16),
            pltpu.VMEM((blocks, hours, tile), F32),
            pltpu.VMEM((blocks, hours, tile), BF16),
            pltpu.VMEM((n, hours, tile), BF16),
            pltpu.VMEM((n, hours, tile), BF16),
            pltpu.VMEM((n, hours, tile), BF16),
            pltpu.VMEM((n, hours, tile), BF16),
            pltpu.SMEM((1, n), jnp.int32),
            pltpu.VMEM((n, 1, tile), jnp.int32),
            pltpu.VMEM((n, 1, tile), jnp.int32),
            pltpu.SMEM((n, 1, tile), jnp.int32),
            pltpu.SemaphoreType.DMA((10,)),
            pltpu.SemaphoreType.DMA((loads,)),
            pltpu.SemaphoreType.DMA((2,)),
            pltpu.SemaphoreType.DMA((3, n)),
            pltpu.SemaphoreType.DMA((3, n)),
        ],
        compiler_params=pltpu.CompilerParams(
            collective_id=0, has_side_effects=True, vmem_limit_bytes=24 * 2**20
        ),
    )(
        *(
            pltpu.with_memory_space_constraint(a, pltpu.HBM)
            for a in (
                sky_radiance,
                surf_coeff.reshape(blocks, depth, tile),
                surf_patch.T,
                surf_count,
                sens_coeff.reshape(sens_blocks, depth, tile),
                sens_patch.T,
                sens_count,
                albedo.reshape(blocks, 1, tile),
                view_tile.reshape(blocks, depth, tile),
                view_peer.T,
                wanted.reshape(1, 1, n),
                sens_surf,
                sens_weight,
            )
        )
    )
    return sensors(*made)


def near(
    parts,
    surf,
    sens,
    refl,
    most,
    onehot,
    place,
    weight,
    surf_hbm,
    sens_hbm,
    out,
    pieces,
    sem,
):
    hours, width = refl.shape
    tile = onehot.shape[2] // 2
    stores = [pltpu.make_async_copy(surf, surf_hbm, sem.at[0])]
    stores[0].start()

    top = jnp.max(jnp.max(most[...], axis=0, keepdims=True), axis=1, keepdims=True)
    rest = refl[...] * (TOP / top)
    for i in range(3):
        piece = rest.astype(F8)
        pieces[i * hours : (i + 1) * hours, :] = piece
        rest = (rest - piece.astype(F32)) * STEP
    back = top * (1 / TOP)

    def by_matmul(cols, r):
        found = jnp.dot(pieces[...], onehot[r], preferred_element_type=F32)
        found = found[:hours] + (1 / STEP) * (
            found[hours : 2 * hours] + (1 / STEP) * found[2 * hours :]
        )
        gain = weight[:, cols] * back
        out[:, cols] = (
            sens[:, cols] + gain[0:1] * found[:, :tile] + gain[1:2] * found[:, tile:]
        )

    def by_gather(cols):
        block = place[:, cols] // tile
        lane = place[:, cols] - block * tile
        rows = 8
        shape = (rows, tile)
        for h in range(0, hours, rows):
            total = sens[h : h + rows, cols]
            for j in range(2):
                lanes = jnp.broadcast_to(lane[j : j + 1], shape)
                picked = jnp.broadcast_to(block[j : j + 1], shape)
                found = jnp.zeros(shape, F32)
                for s in range(width // tile):
                    part = refl[h : h + rows, s * tile : (s + 1) * tile]
                    part = jnp.take_along_axis(part, lanes, axis=1)
                    found = jnp.where(picked == s, part, found)
                total = total + jnp.broadcast_to(weight[j : j + 1, cols], shape) * found
            out[h : h + rows, cols] = total

    low = 0
    for i, high in enumerate(parts):
        for r in range(low, high):
            cols = pl.ds(r * tile, tile)
            if r == 0 or (r % 4 == 3 and r < parts[-1] - 4):
                by_gather(cols)
            else:
                by_matmul(cols, r)
        cols = pl.ds(low * tile, (high - low) * tile)
        copy = pltpu.make_async_copy(out.at[:, cols], sens_hbm.at[:, cols], sem.at[1 + i])
        copy.start()
        stores.append(copy)
        low = high
    for copy in stores:
        copy.wait()


def sensors(*arrays):
    surf, sens, refl = arrays[:3]
    hours, width = refl.shape
    count = arrays[4].shape[0]
    parts = [*range(6, count - 5, 6), count - 2, count] if count > 6 else [count]
    hbm = pl.BlockSpec(memory_space=pltpu.HBM)
    vmem = pl.BlockSpec(memory_space=pltpu.VMEM)
    return pl.pallas_call(
        functools.partial(near, parts),
        out_shape=(
            jax.ShapeDtypeStruct(surf.shape, F32),
            jax.ShapeDtypeStruct(sens.shape, F32),
        ),
        in_specs=[vmem] * 7,
        out_specs=(hbm, hbm),
        scratch_shapes=[
            pltpu.VMEM(sens.shape, F32),
            pltpu.VMEM((3 * hours, width), F8),
            pltpu.SemaphoreType.DMA((1 + len(parts),)),
        ],
        compiler_params=pltpu.CompilerParams(vmem_limit_bytes=8 * 2**20),
    )(*(pltpu.with_memory_space_constraint(a, pltpu.VMEM) for a in arrays))


def solution(mesh):
    in_specs = (
        P("hours", None),
        P("surf", None, None, None),
        P("surf", None),
        P("surf"),
        P("surf", None, None, None),
        P("surf", None),
        P("surf"),
        P("surf"),
        P("surf", None, None, None),
        P("surf", None),
        P("surf", None),
        P(None, "surf"),
        P(None, "surf"),
    )
    out_specs = (P("hours", "surf"), P("hours", "surf"))
    return jax.shard_map(local, mesh=mesh, in_specs=in_specs, out_specs=out_specs, check_vma=False)
```

```python
import functools

import jax
import jax.numpy as jnp
from jax import lax
from jax.experimental import pallas as pl
from jax.experimental.pallas import tpu as pltpu
from jax.sharding import PartitionSpec as P

F32 = jnp.float32
BF16 = jnp.bfloat16
F8 = jnp.float8_e4m3fn

TOP = 256.0
STEP = 32.0


def wide_dot(table, picks, weights):
    lhs = jnp.concatenate([table[i] for i in picks], axis=1)
    return jnp.dot(lhs, weights, preferred_element_type=F32)


def farthest_first(n):
    if n > 8 or n & (n - 1):
        return None
    return [*range(n - 1, 0, -2), *range(n - 2, 0, -2)]


def kernel(
    n,
    sky_hbm,
    surf_hbm,
    surf_patch_hbm,
    surf_count_hbm,
    sens_hbm,
    sens_patch_hbm,
    sens_count_hbm,
    albedo_hbm,
    view_hbm,
    view_peer_hbm,
    wanted_hbm,
    sens_surf_hbm,
    sens_weight_hbm,
    surf_out,
    sens_out,
    refl,
    most,
    onehot,
    place,
    weight,
    sky,
    surf_patch,
    surf_count,
    sens_patch,
    sens_count,
    albedo,
    view_peer,
    sens_surf,
    sky_tab,
    surf_w,
    sens_w,
    view_w,
    direct,
    rad,
    send_a,
    send_b,
    slots_a,
    slots_b,
    want_own,
    want_rows,
    want_v,
    want_s,
    small_sem,
    load_sem,
    want_sem,
    send_sem,
    recv_sem,
):
    hours, patch_width = sky.shape
    blocks, depth, tile = view_w.shape
    sens_blocks = sens_w.shape[0]
    per = depth // tile
    patches = patch_width // tile
    me = lax.axis_index("surf")
    far = farthest_first(n)

    def out_to(step):
        if far is None:
            return lax.rem(me + step, n)
        to = me
        for bit in (1, 2, 4):
            if step & bit:
                to = to + bit * (1 - 2 * lax.rem(me // bit, 2))
        return to

    def in_from(step):
        return lax.rem(me + n - step, n) if far is None else out_to(step)

    barrier = pltpu.get_barrier_semaphore()

    def loop(low, high, body, group):
        count = high - low
        group = next(g for g in range(min(group, count), 0, -1) if count % g == 0)

        def go(i, carry):
            for u in range(group):
                body(low + i * group + u)
            return carry

        lax.fori_loop(0, count // group, go, 0)

    def each(turn, body):
        if far is None:
            loop(1, n, lambda step: body(turn(step)), 7)
        else:
            for step in range(1, n):
                body(turn(step))

    def each_far(body):
        if far is None:
            each(out_to, body)
        else:
            for step in far:
                body(out_to(step))

    def greet(peer):
        pl.semaphore_signal(
            barrier, inc=1, device_id={"surf": peer}, device_id_type=pl.DeviceIdType.MESH
        )

    each_far(greet)

    surf_parts = load_parts(blocks)
    sens_parts = load_parts(sens_blocks)

    def part(hbm, vmem, parts, i, first):
        size = vmem.shape[0] // parts
        span = pl.ds(i * size, size)
        return pltpu.make_async_copy(hbm.at[span], vmem.at[span], load_sem.at[first + i])

    surf_loads = [part(surf_hbm, surf_w, surf_parts, i, 0) for i in range(surf_parts)]
    view_load = part(view_hbm, view_w, 1, 0, surf_parts)
    sens_loads = [
        part(sens_hbm, sens_w, sens_parts, i, surf_parts + 1) for i in range(sens_parts)
    ]
    small = (
        (wanted_hbm.at[0], want_own),
        (sky_hbm, sky),
        (surf_patch_hbm, surf_patch),
        (surf_count_hbm, surf_count),
        (albedo_hbm, albedo),
        (view_peer_hbm, view_peer),
        (sens_patch_hbm, sens_patch),
        (sens_count_hbm, sens_count),
        (sens_surf_hbm, sens_surf),
        (sens_weight_hbm, weight),
    )
    small_loads = [
        pltpu.make_async_copy(src, dst, small_sem.at[i]) for i, (src, dst) in enumerate(small)
    ]
    early, late = small_loads[:5], small_loads[5:]
    for copy in (*early, *surf_loads, *late):
        copy.start()

    def remote(src, dst, kind, to, mine):
        return pltpu.make_async_remote_copy(
            src_ref=src,
            dst_ref=dst.at[mine],
            send_sem=send_sem.at[kind, to],
            recv_sem=recv_sem.at[kind, mine],
            device_id={"surf": to},
            device_id_type=pl.DeviceIdType.MESH,
        )

    early[0].wait()
    for e in range(n):
        want_rows[e] = jnp.full(want_rows.shape[1:], want_own[0, e], jnp.int32)
    want_v[me] = want_rows[me]
    pl.semaphore_wait(barrier, n - 1)
    each_far(lambda e: remote(want_rows.at[e], want_v, 0, e, me).start())

    early[1].wait()
    for j in range(patches):
        sky_tab[j] = sky[:, j * tile : (j + 1) * tile]
    sky_tab[patches] = jnp.zeros((hours, tile), BF16)

    def live(patch, count, k, b):
        return jnp.where(k < count[b], patch[k, b], patches)

    def direct_block(b):
        picks = [live(surf_patch, surf_count, k, b) for k in range(per)]
        value = wide_dot(sky_tab, picks, surf_w[b])
        direct[b] = value
        rad[b] = (value * albedo[b]).astype(BF16)

    def sens_block(b):
        picks = [live(sens_patch, sens_count, k, b) for k in range(per)]
        cols = pl.ds(pl.multiple_of(b * tile, tile), tile)
        sens_out[:, cols] = wide_dot(sky_tab, picks, sens_w[b])

    for copy in early[2:]:
        copy.wait()
    for i, copy in enumerate(surf_loads):
        copy.wait()
        size = blocks // surf_parts
        loop(i * size, (i + 1) * size, direct_block, 4)

    for copy in late:
        copy.wait()
    for copy in (*sens_loads[:2], view_load, *sens_loads[2:]):
        copy.start()
    place[...] = sens_surf[...] - me * (blocks * tile)

    def first_send(e):
        remote(want_rows.at[e], want_v, 0, me, e).wait_recv()
        send_a[e] = rad[jnp.max(want_v[e])]
        remote(send_a.at[e], slots_a, 1, e, me).start()

    each(in_from, first_send)
    slots_a[me] = rad[jnp.max(want_v[me])]
    to_smem = pltpu.make_async_copy(want_v, want_s, want_sem.at[0])
    to_smem.start()

    half = sens_parts // 2
    rows = lax.broadcasted_iota(jnp.int32, (tile, 2 * tile), 0).astype(jnp.int16)
    ones = jnp.ones((tile, 2 * tile), BF16)
    zeros = jnp.zeros((tile, 2 * tile), BF16)

    def onehot_block(r):
        cols = pl.ds(pl.multiple_of(r * tile, tile), tile)
        index = place[:, cols]
        index = jnp.concatenate([index[0:1], index[1:2]], axis=1)
        index = jnp.broadcast_to(index, (tile, 2 * tile)).astype(jnp.int16)
        for s in range(blocks):
            hit = rows == index - jnp.int16(s * tile)
            onehot[r, s * tile : (s + 1) * tile, :] = jnp.where(hit, ones, zeros).astype(F8)

    def sens_part(i):
        sens_loads[i].wait()
        size = sens_blocks // sens_parts
        loop(i * size, (i + 1) * size, sens_block, 6)
        loop(i * size, (i + 1) * size, onehot_block, 1)

    for i in range(half):
        sens_part(i)

    view_load.wait()
    to_smem.wait()
    each(in_from, lambda e: remote(send_a.at[e], slots_a, 1, me, e).wait_recv())

    def bounced(slots, b):
        picks = [view_peer[k, b] for k in range(per)]
        return wide_dot(slots, picks, view_w[b])

    def asked(e):
        return want_s[e, 0, 0]

    def second_value(b):
        value = direct[b] + bounced(slots_a, b)
        return (value * albedo[b]).astype(BF16)

    def second_send(e):
        send_b[e] = second_value(asked(e))
        remote(send_b.at[e], slots_b, 2, e, me).start()

    if far is None:
        each_far(second_send)
    else:
        peers = [out_to(step) for step in far]
        cuts = sorted({0, *(c for c in (2, 4) if c < n - 1), n - 1})
        for low, high in zip(cuts, cuts[1:]):
            values = [second_value(asked(e)) for e in peers[low:high]]
            for e, value in zip(peers[low:high], values):
                send_b[e] = value
            for e in peers[low:high]:
                remote(send_b.at[e], slots_b, 2, e, me).start()
    slots_b[me] = second_value(asked(me))

    for i in range(half, sens_parts):
        sens_part(i)

    each(out_to, lambda e: remote(want_rows.at[e], want_v, 0, e, me).wait_send())
    each(out_to, lambda e: remote(send_a.at[e], slots_a, 1, e, me).wait_send())
    each(in_from, lambda e: remote(send_b.at[e], slots_b, 2, me, e).wait_recv())

    group = next(g for g in (16, 8, 4, 2, 1) if blocks % g == 0)

    def last_blocks(i, top):
        for u in range(group):
            b = i * group + u
            value = bounced(slots_b, b)
            cols = pl.ds(pl.multiple_of(b * tile, tile), tile)
            refl[:, cols] = value
            surf_out[:, cols] = direct[b] + value
            top = jnp.maximum(top, jnp.abs(value))
        return top

    most[...] = lax.fori_loop(0, blocks // group, last_blocks, jnp.full((hours, tile), 1e-30, F32))

    each(out_to, lambda e: remote(send_b.at[e], slots_b, 2, e, me).wait_send())


def load_parts(blocks):
    return 4 if blocks % 4 == 0 else 1


def local(
    sky_radiance,
    surf_coeff,
    surf_patch,
    surf_count,
    sens_coeff,
    sens_patch,
    sens_count,
    albedo,
    view_tile,
    view_peer,
    wanted,
    sens_surf,
    sens_weight,
):
    n = lax.axis_size("surf")
    hours, patch_width = sky_radiance.shape
    blocks, per, tile, _ = view_tile.shape
    sens_blocks = sens_coeff.shape[0]
    depth = per * tile
    patches = patch_width // tile

    hbm = pl.BlockSpec(memory_space=pltpu.HBM)
    vmem = pl.BlockSpec(memory_space=pltpu.VMEM)
    loads = load_parts(blocks) + 1 + load_parts(sens_blocks)
    made = pl.pallas_call(
        functools.partial(kernel, n),
        out_shape=(
            pltpu.VMEM((hours, blocks * tile), F32),
            pltpu.VMEM((hours, sens_blocks * tile), F32),
            pltpu.VMEM((hours, blocks * tile), F32),
            pltpu.VMEM((hours, tile), F32),
            pltpu.VMEM((sens_blocks, blocks * tile, 2 * tile), F8),
            pltpu.VMEM(sens_surf.shape, jnp.int32),
            pltpu.VMEM(sens_weight.shape, F32),
        ),
        in_specs=[hbm] * 13,
        out_specs=(vmem,) * 7,
        scratch_shapes=[
            pltpu.VMEM((hours, patch_width), BF16),
            pltpu.SMEM((per, blocks), jnp.int32),
            pltpu.SMEM((blocks,), jnp.int32),
            pltpu.SMEM((per, sens_blocks), jnp.int32),
            pltpu.SMEM((sens_blocks,), jnp.int32),
            pltpu.VMEM((blocks, 1, tile), F32),
            pltpu.SMEM((per, blocks), jnp.int32),
            pltpu.VMEM(sens_surf.shape, jnp.int32),
            pltpu.VMEM((patches + 1, hours, tile), BF16),
            pltpu.VMEM((blocks, depth, tile), BF16),
            pltpu.VMEM((sens_blocks, depth, tile), BF16),
            pltpu.VMEM((blocks, depth, tile), BF16),
            pltpu.VMEM((blocks, hours, tile), F32),
            pltpu.VMEM((blocks, hours, tile), BF16),
            pltpu.VMEM((n, hours, tile), BF16),
            pltpu.VMEM((n, hours, tile), BF16),
            pltpu.VMEM((n, hours, tile), BF16),
            pltpu.VMEM((n, hours, tile), BF16),
            pltpu.SMEM((1, n), jnp.int32),
            pltpu.VMEM((n, 1, tile), jnp.int32),
            pltpu.VMEM((n, 1, tile), jnp.int32),
            pltpu.SMEM((n, 1, tile), jnp.int32),
            pltpu.SemaphoreType.DMA((10,)),
            pltpu.SemaphoreType.DMA((loads,)),
            pltpu.SemaphoreType.DMA((2,)),
            pltpu.SemaphoreType.DMA((3, n)),
            pltpu.SemaphoreType.DMA((3, n)),
        ],
        compiler_params=pltpu.CompilerParams(
            collective_id=0, has_side_effects=True, vmem_limit_bytes=24 * 2**20
        ),
    )(
        *(
            pltpu.with_memory_space_constraint(a, pltpu.HBM)
            for a in (
                sky_radiance,
                surf_coeff.reshape(blocks, depth, tile),
                surf_patch.T,
                surf_count,
                sens_coeff.reshape(sens_blocks, depth, tile),
                sens_patch.T,
                sens_count,
                albedo.reshape(blocks, 1, tile),
                view_tile.reshape(blocks, depth, tile),
                view_peer.T,
                wanted.reshape(1, 1, n),
                sens_surf,
                sens_weight,
            )
        )
    )
    return sensors(*made)


def near(
    parts,
    surf,
    sens,
    refl,
    most,
    onehot,
    place,
    weight,
    surf_hbm,
    sens_hbm,
    out,
    pieces,
    sem,
):
    hours, width = refl.shape
    tile = onehot.shape[2] // 2
    stores = [pltpu.make_async_copy(surf, surf_hbm, sem.at[0])]
    stores[0].start()

    top = jnp.max(jnp.max(most[...], axis=0, keepdims=True), axis=1, keepdims=True)
    rest = refl[...] * (TOP / top)
    for i in range(3):
        piece = rest.astype(F8)
        pieces[i * hours : (i + 1) * hours, :] = piece
        rest = (rest - piece.astype(F32)) * STEP
    back = top * (1 / TOP)

    def by_matmul(cols, r):
        found = jnp.dot(pieces[...], onehot[r], preferred_element_type=F32)
        found = found[:hours] + (1 / STEP) * (
            found[hours : 2 * hours] + (1 / STEP) * found[2 * hours :]
        )
        gain = weight[:, cols] * back
        out[:, cols] = (
            sens[:, cols] + gain[0:1] * found[:, :tile] + gain[1:2] * found[:, tile:]
        )

    def by_gather(cols):
        block = place[:, cols] // tile
        lane = place[:, cols] - block * tile
        rows = 8
        shape = (rows, tile)
        for h in range(0, hours, rows):
            total = sens[h : h + rows, cols]
            for j in range(2):
                lanes = jnp.broadcast_to(lane[j : j + 1], shape)
                picked = jnp.broadcast_to(block[j : j + 1], shape)
                found = jnp.zeros(shape, F32)
                for s in range(width // tile):
                    part = refl[h : h + rows, s * tile : (s + 1) * tile]
                    part = jnp.take_along_axis(part, lanes, axis=1)
                    found = jnp.where(picked == s, part, found)
                total = total + jnp.broadcast_to(weight[j : j + 1, cols], shape) * found
            out[h : h + rows, cols] = total

    low = 0
    for i, high in enumerate(parts):
        for r in range(low, high):
            cols = pl.ds(r * tile, tile)
            if r == 0 or (r % 4 == 3 and r < parts[-1] - 4):
                by_gather(cols)
            else:
                by_matmul(cols, r)
        cols = pl.ds(low * tile, (high - low) * tile)
        copy = pltpu.make_async_copy(out.at[:, cols], sens_hbm.at[:, cols], sem.at[1 + i])
        copy.start()
        stores.append(copy)
        low = high
    for copy in stores:
        copy.wait()


def sensors(*arrays):
    surf, sens, refl = arrays[:3]
    hours, width = refl.shape
    count = arrays[4].shape[0]
    parts = [*range(6, count - 5, 6), count - 2, count] if count > 6 else [count]
    hbm = pl.BlockSpec(memory_space=pltpu.HBM)
    vmem = pl.BlockSpec(memory_space=pltpu.VMEM)
    return pl.pallas_call(
        functools.partial(near, parts),
        out_shape=(
            jax.ShapeDtypeStruct(surf.shape, F32),
            jax.ShapeDtypeStruct(sens.shape, F32),
        ),
        in_specs=[vmem] * 7,
        out_specs=(hbm, hbm),
        scratch_shapes=[
            pltpu.VMEM(sens.shape, F32),
            pltpu.VMEM((3 * hours, width), F8),
            pltpu.SemaphoreType.DMA((1 + len(parts),)),
        ],
        compiler_params=pltpu.CompilerParams(vmem_limit_bytes=8 * 2**20),
    )(*(pltpu.with_memory_space_constraint(a, pltpu.VMEM) for a in arrays))


def solution(mesh):
    in_specs = (
        P("hours", None),
        P("surf", None, None, None),
        P("surf", None),
        P("surf"),
        P("surf", None, None, None),
        P("surf", None),
        P("surf"),
        P("surf"),
        P("surf", None, None, None),
        P("surf", None),
        P("surf", None),
        P(None, "surf"),
        P(None, "surf"),
    )
    out_specs = (P("hours", "surf"), P("hours", "surf"))
    return jax.shard_map(local, mesh=mesh, in_specs=in_specs, out_specs=out_specs, check_vma=False)
```

```python
import functools

import jax
import jax.numpy as jnp
from jax import lax
from jax.experimental import pallas as pl
from jax.experimental.pallas import tpu as pltpu
from jax.sharding import PartitionSpec as P

F32 = jnp.float32
BF16 = jnp.bfloat16
F8 = jnp.float8_e4m3fn

TOP = 256.0
STEP = 32.0


def wide_dot(table, picks, weights):
    lhs = jnp.concatenate([table[i] for i in picks], axis=1)
    return jnp.dot(lhs, weights, preferred_element_type=F32)


def farthest_first(n):
    if n > 8 or n & (n - 1):
        return None
    return [*range(n - 1, 0, -1)]


def kernel(
    n,
    sky_hbm,
    surf_hbm,
    surf_patch_hbm,
    surf_count_hbm,
    sens_hbm,
    sens_patch_hbm,
    sens_count_hbm,
    albedo_hbm,
    view_hbm,
    view_peer_hbm,
    wanted_hbm,
    sens_surf_hbm,
    sens_weight_hbm,
    surf_out,
    sens_out,
    refl,
    most,
    onehot,
    place,
    weight,
    sky,
    surf_patch,
    surf_count,
    sens_patch,
    sens_count,
    albedo,
    view_peer,
    sens_surf,
    sky_tab,
    surf_w,
    sens_w,
    view_w,
    direct,
    rad,
    send_a,
    send_b,
    slots_a,
    slots_b,
    want_own,
    want_rows,
    want_v,
    want_s,
    small_sem,
    load_sem,
    want_sem,
    send_sem,
    recv_sem,
):
    hours, patch_width = sky.shape
    blocks, depth, tile = view_w.shape
    sens_blocks = sens_w.shape[0]
    per = depth // tile
    patches = patch_width // tile
    me = lax.axis_index("surf")
    far = farthest_first(n)

    def out_to(step):
        if far is None:
            return lax.rem(me + step, n)
        to = me
        for bit in (1, 2, 4):
            if step & bit:
                to = to + bit * (1 - 2 * lax.rem(me // bit, 2))
        return to

    def in_from(step):
        return lax.rem(me + n - step, n) if far is None else out_to(step)

    barrier = pltpu.get_barrier_semaphore()

    def loop(low, high, body, group):
        count = high - low
        group = next(g for g in range(min(group, count), 0, -1) if count % g == 0)

        def go(i, carry):
            for u in range(group):
                body(low + i * group + u)
            return carry

        lax.fori_loop(0, count // group, go, 0)

    def each(turn, body):
        if far is None:
            loop(1, n, lambda step: body(turn(step)), 7)
        else:
            for step in range(1, n):
                body(turn(step))

    def each_far(body):
        if far is None:
            each(out_to, body)
        else:
            for step in far:
                body(out_to(step))

    def greet(peer):
        pl.semaphore_signal(
            barrier, inc=1, device_id={"surf": peer}, device_id_type=pl.DeviceIdType.MESH
        )

    each_far(greet)

    surf_parts = load_parts(blocks)
    sens_parts = load_parts(sens_blocks)

    def part(hbm, vmem, parts, i, first):
        size = vmem.shape[0] // parts
        span = pl.ds(i * size, size)
        return pltpu.make_async_copy(hbm.at[span], vmem.at[span], load_sem.at[first + i])

    surf_loads = [part(surf_hbm, surf_w, surf_parts, i, 0) for i in range(surf_parts)]
    view_load = part(view_hbm, view_w, 1, 0, surf_parts)
    sens_loads = [
        part(sens_hbm, sens_w, sens_parts, i, surf_parts + 1) for i in range(sens_parts)
    ]
    small = (
        (wanted_hbm.at[0], want_own),
        (sky_hbm, sky),
        (surf_patch_hbm, surf_patch),
        (surf_count_hbm, surf_count),
        (albedo_hbm, albedo),
        (view_peer_hbm, view_peer),
        (sens_patch_hbm, sens_patch),
        (sens_count_hbm, sens_count),
        (sens_surf_hbm, sens_surf),
        (sens_weight_hbm, weight),
    )
    small_loads = [
        pltpu.make_async_copy(src, dst, small_sem.at[i]) for i, (src, dst) in enumerate(small)
    ]
    early, late = small_loads[:5], small_loads[5:]
    for copy in (*early, *surf_loads, *late):
        copy.start()

    def remote(src, dst, kind, to, mine):
        return pltpu.make_async_remote_copy(
            src_ref=src,
            dst_ref=dst.at[mine],
            send_sem=send_sem.at[kind, to],
            recv_sem=recv_sem.at[kind, mine],
            device_id={"surf": to},
            device_id_type=pl.DeviceIdType.MESH,
        )

    early[0].wait()
    for e in range(n):
        want_rows[e] = jnp.full(want_rows.shape[1:], want_own[0, e], jnp.int32)
    want_v[me] = want_rows[me]
    pl.semaphore_wait(barrier, n - 1)
    each_far(lambda e: remote(want_rows.at[e], want_v, 0, e, me).start())

    early[1].wait()
    for j in range(patches):
        sky_tab[j] = sky[:, j * tile : (j + 1) * tile]
    sky_tab[patches] = jnp.zeros((hours, tile), BF16)

    def live(patch, count, k, b):
        return jnp.where(k < count[b], patch[k, b], patches)

    def direct_block(b):
        picks = [live(surf_patch, surf_count, k, b) for k in range(per)]
        value = wide_dot(sky_tab, picks, surf_w[b])
        direct[b] = value
        rad[b] = (value * albedo[b]).astype(BF16)

    def sens_block(b):
        picks = [live(sens_patch, sens_count, k, b) for k in range(per)]
        cols = pl.ds(pl.multiple_of(b * tile, tile), tile)
        sens_out[:, cols] = wide_dot(sky_tab, picks, sens_w[b])

    for copy in early[2:]:
        copy.wait()
    for i, copy in enumerate(surf_loads):
        copy.wait()
        size = blocks // surf_parts
        loop(i * size, (i + 1) * size, direct_block, 4)

    for copy in late:
        copy.wait()
    for copy in (*sens_loads[:2], view_load, *sens_loads[2:]):
        copy.start()
    place[...] = sens_surf[...] - me * (blocks * tile)

    def first_send(e):
        remote(want_rows.at[e], want_v, 0, me, e).wait_recv()
        send_a[e] = rad[jnp.max(want_v[e])]
        remote(send_a.at[e], slots_a, 1, e, me).start()

    each(in_from, first_send)
    slots_a[me] = rad[jnp.max(want_v[me])]
    to_smem = pltpu.make_async_copy(want_v, want_s, want_sem.at[0])
    to_smem.start()

    half = sens_parts // 2
    rows = lax.broadcasted_iota(jnp.int32, (tile, 2 * tile), 0).astype(jnp.int16)
    ones = jnp.ones((tile, 2 * tile), BF16)
    zeros = jnp.zeros((tile, 2 * tile), BF16)

    def onehot_block(r):
        cols = pl.ds(pl.multiple_of(r * tile, tile), tile)
        index = place[:, cols]
        index = jnp.concatenate([index[0:1], index[1:2]], axis=1)
        index = jnp.broadcast_to(index, (tile, 2 * tile)).astype(jnp.int16)
        for s in range(blocks):
            hit = rows == index - jnp.int16(s * tile)
            onehot[r, s * tile : (s + 1) * tile, :] = jnp.where(hit, ones, zeros).astype(F8)

    def sens_part(i):
        sens_loads[i].wait()
        size = sens_blocks // sens_parts
        loop(i * size, (i + 1) * size, sens_block, 6)
        loop(i * size, (i + 1) * size, onehot_block, 1)

    for i in range(half):
        sens_part(i)

    view_load.wait()
    to_smem.wait()
    each(in_from, lambda e: remote(send_a.at[e], slots_a, 1, me, e).wait_recv())

    def bounced(slots, b):
        picks = [view_peer[k, b] for k in range(per)]
        return wide_dot(slots, picks, view_w[b])

    def asked(e):
        return want_s[e, 0, 0]

    def second_value(b):
        value = direct[b] + bounced(slots_a, b)
        return (value * albedo[b]).astype(BF16)

    def second_send(e):
        send_b[e] = second_value(asked(e))
        remote(send_b.at[e], slots_b, 2, e, me).start()

    if far is None:
        each_far(second_send)
    else:
        peers = [out_to(step) for step in far]
        cuts = sorted({0, *(c for c in (2, 4) if c < n - 1), n - 1})
        for low, high in zip(cuts, cuts[1:]):
            values = [second_value(asked(e)) for e in peers[low:high]]
            for e, value in zip(peers[low:high], values):
                send_b[e] = value
            for e in peers[low:high]:
                remote(send_b.at[e], slots_b, 2, e, me).start()
    slots_b[me] = second_value(asked(me))

    for i in range(half, sens_parts):
        sens_part(i)

    each(out_to, lambda e: remote(want_rows.at[e], want_v, 0, e, me).wait_send())
    each(out_to, lambda e: remote(send_a.at[e], slots_a, 1, e, me).wait_send())
    each(in_from, lambda e: remote(send_b.at[e], slots_b, 2, me, e).wait_recv())

    group = next(g for g in (16, 8, 4, 2, 1) if blocks % g == 0)

    def last_blocks(i, top):
        for u in range(group):
            b = i * group + u
            value = bounced(slots_b, b)
            cols = pl.ds(pl.multiple_of(b * tile, tile), tile)
            refl[:, cols] = value
            surf_out[:, cols] = direct[b] + value
            top = jnp.maximum(top, jnp.abs(value))
        return top

    most[...] = lax.fori_loop(0, blocks // group, last_blocks, jnp.full((hours, tile), 1e-30, F32))

    each(out_to, lambda e: remote(send_b.at[e], slots_b, 2, e, me).wait_send())


def load_parts(blocks):
    return 4 if blocks % 4 == 0 else 1


def local(
    sky_radiance,
    surf_coeff,
    surf_patch,
    surf_count,
    sens_coeff,
    sens_patch,
    sens_count,
    albedo,
    view_tile,
    view_peer,
    wanted,
    sens_surf,
    sens_weight,
):
    n = lax.axis_size("surf")
    hours, patch_width = sky_radiance.shape
    blocks, per, tile, _ = view_tile.shape
    sens_blocks = sens_coeff.shape[0]
    depth = per * tile
    patches = patch_width // tile

    hbm = pl.BlockSpec(memory_space=pltpu.HBM)
    vmem = pl.BlockSpec(memory_space=pltpu.VMEM)
    loads = load_parts(blocks) + 1 + load_parts(sens_blocks)
    made = pl.pallas_call(
        functools.partial(kernel, n),
        out_shape=(
            pltpu.VMEM((hours, blocks * tile), F32),
            pltpu.VMEM((hours, sens_blocks * tile), F32),
            pltpu.VMEM((hours, blocks * tile), F32),
            pltpu.VMEM((hours, tile), F32),
            pltpu.VMEM((sens_blocks, blocks * tile, 2 * tile), F8),
            pltpu.VMEM(sens_surf.shape, jnp.int32),
            pltpu.VMEM(sens_weight.shape, F32),
        ),
        in_specs=[hbm] * 13,
        out_specs=(vmem,) * 7,
        scratch_shapes=[
            pltpu.VMEM((hours, patch_width), BF16),
            pltpu.SMEM((per, blocks), jnp.int32),
            pltpu.SMEM((blocks,), jnp.int32),
            pltpu.SMEM((per, sens_blocks), jnp.int32),
            pltpu.SMEM((sens_blocks,), jnp.int32),
            pltpu.VMEM((blocks, 1, tile), F32),
            pltpu.SMEM((per, blocks), jnp.int32),
            pltpu.VMEM(sens_surf.shape, jnp.int32),
            pltpu.VMEM((patches + 1, hours, tile), BF16),
            pltpu.VMEM((blocks, depth, tile), BF16),
            pltpu.VMEM((sens_blocks, depth, tile), BF16),
            pltpu.VMEM((blocks, depth, tile), BF16),
            pltpu.VMEM((blocks, hours, tile), F32),
            pltpu.VMEM((blocks, hours, tile), BF16),
            pltpu.VMEM((n, hours, tile), BF16),
            pltpu.VMEM((n, hours, tile), BF16),
            pltpu.VMEM((n, hours, tile), BF16),
            pltpu.VMEM((n, hours, tile), BF16),
            pltpu.SMEM((1, n), jnp.int32),
            pltpu.VMEM((n, 1, tile), jnp.int32),
            pltpu.VMEM((n, 1, tile), jnp.int32),
            pltpu.SMEM((n, 1, tile), jnp.int32),
            pltpu.SemaphoreType.DMA((10,)),
            pltpu.SemaphoreType.DMA((loads,)),
            pltpu.SemaphoreType.DMA((2,)),
            pltpu.SemaphoreType.DMA((3, n)),
            pltpu.SemaphoreType.DMA((3, n)),
        ],
        compiler_params=pltpu.CompilerParams(
            collective_id=0, has_side_effects=True, vmem_limit_bytes=24 * 2**20
        ),
    )(
        *(
            pltpu.with_memory_space_constraint(a, pltpu.HBM)
            for a in (
                sky_radiance,
                surf_coeff.reshape(blocks, depth, tile),
                surf_patch.T,
                surf_count,
                sens_coeff.reshape(sens_blocks, depth, tile),
                sens_patch.T,
                sens_count,
                albedo.reshape(blocks, 1, tile),
                view_tile.reshape(blocks, depth, tile),
                view_peer.T,
                wanted.reshape(1, 1, n),
                sens_surf,
                sens_weight,
            )
        )
    )
    return sensors(*made)


def near(
    parts,
    surf,
    sens,
    refl,
    most,
    onehot,
    place,
    weight,
    surf_hbm,
    sens_hbm,
    out,
    pieces,
    sem,
):
    hours, width = refl.shape
    tile = onehot.shape[2] // 2
    stores = [pltpu.make_async_copy(surf, surf_hbm, sem.at[0])]
    stores[0].start()

    top = jnp.max(jnp.max(most[...], axis=0, keepdims=True), axis=1, keepdims=True)
    rest = refl[...] * (TOP / top)
    for i in range(3):
        piece = rest.astype(F8)
        pieces[i * hours : (i + 1) * hours, :] = piece
        rest = (rest - piece.astype(F32)) * STEP
    back = top * (1 / TOP)

    def by_matmul(cols, r):
        found = jnp.dot(pieces[...], onehot[r], preferred_element_type=F32)
        found = found[:hours] + (1 / STEP) * (
            found[hours : 2 * hours] + (1 / STEP) * found[2 * hours :]
        )
        gain = weight[:, cols] * back
        out[:, cols] = (
            sens[:, cols] + gain[0:1] * found[:, :tile] + gain[1:2] * found[:, tile:]
        )

    def by_gather(cols):
        block = place[:, cols] // tile
        lane = place[:, cols] - block * tile
        rows = 8
        shape = (rows, tile)
        for h in range(0, hours, rows):
            total = sens[h : h + rows, cols]
            for j in range(2):
                lanes = jnp.broadcast_to(lane[j : j + 1], shape)
                picked = jnp.broadcast_to(block[j : j + 1], shape)
                found = jnp.zeros(shape, F32)
                for s in range(width // tile):
                    part = refl[h : h + rows, s * tile : (s + 1) * tile]
                    part = jnp.take_along_axis(part, lanes, axis=1)
                    found = jnp.where(picked == s, part, found)
                total = total + jnp.broadcast_to(weight[j : j + 1, cols], shape) * found
            out[h : h + rows, cols] = total

    low = 0
    for i, high in enumerate(parts):
        for r in range(low, high):
            cols = pl.ds(r * tile, tile)
            if r == 0 or (r % 4 == 3 and r < parts[-1] - 4):
                by_gather(cols)
            else:
                by_matmul(cols, r)
        cols = pl.ds(low * tile, (high - low) * tile)
        copy = pltpu.make_async_copy(out.at[:, cols], sens_hbm.at[:, cols], sem.at[1 + i])
        copy.start()
        stores.append(copy)
        low = high
    for copy in stores:
        copy.wait()


def sensors(*arrays):
    surf, sens, refl = arrays[:3]
    hours, width = refl.shape
    count = arrays[4].shape[0]
    parts = [*range(6, count - 5, 6), count - 2, count] if count > 6 else [count]
    hbm = pl.BlockSpec(memory_space=pltpu.HBM)
    vmem = pl.BlockSpec(memory_space=pltpu.VMEM)
    return pl.pallas_call(
        functools.partial(near, parts),
        out_shape=(
            jax.ShapeDtypeStruct(surf.shape, F32),
            jax.ShapeDtypeStruct(sens.shape, F32),
        ),
        in_specs=[vmem] * 7,
        out_specs=(hbm, hbm),
        scratch_shapes=[
            pltpu.VMEM(sens.shape, F32),
            pltpu.VMEM((3 * hours, width), F8),
            pltpu.SemaphoreType.DMA((1 + len(parts),)),
        ],
        compiler_params=pltpu.CompilerParams(vmem_limit_bytes=8 * 2**20),
    )(*(pltpu.with_memory_space_constraint(a, pltpu.VMEM) for a in arrays))


def solution(mesh):
    in_specs = (
        P("hours", None),
        P("surf", None, None, None),
        P("surf", None),
        P("surf"),
        P("surf", None, None, None),
        P("surf", None),
        P("surf"),
        P("surf"),
        P("surf", None, None, None),
        P("surf", None),
        P("surf", None),
        P(None, "surf"),
        P(None, "surf"),
    )
    out_specs = (P("hours", "surf"), P("hours", "surf"))
    return jax.shard_map(local, mesh=mesh, in_specs=in_specs, out_specs=out_specs, check_vma=False)
```

```python
import functools

import jax
import jax.numpy as jnp
from jax import lax
from jax.experimental import pallas as pl
from jax.experimental.pallas import tpu as pltpu
from jax.sharding import PartitionSpec as P

F32 = jnp.float32
BF16 = jnp.bfloat16
F8 = jnp.float8_e4m3fn

TOP = 256.0
STEP = 32.0


def wide_dot(table, picks, weights):
    lhs = jnp.concatenate([table[i] for i in picks], axis=1)
    return jnp.dot(lhs, weights, preferred_element_type=F32)


def farthest_first(n):
    if n > 8 or n & (n - 1):
        return None
    return [*range(n - 1, 0, -1)]


def kernel(
    n,
    sky_hbm,
    surf_hbm,
    surf_patch_hbm,
    surf_count_hbm,
    sens_hbm,
    sens_patch_hbm,
    sens_count_hbm,
    albedo_hbm,
    view_hbm,
    view_peer_hbm,
    wanted_hbm,
    sens_surf_hbm,
    sens_weight_hbm,
    surf_out,
    sens_out,
    refl,
    most,
    onehot,
    place,
    weight,
    sky,
    surf_patch,
    surf_count,
    sens_patch,
    sens_count,
    albedo,
    view_peer,
    sens_surf,
    sky_tab,
    surf_w,
    sens_w,
    view_w,
    direct,
    rad,
    send_a,
    send_b,
    slots_a,
    slots_b,
    want_own,
    want_rows,
    want_v,
    want_s,
    small_sem,
    load_sem,
    want_sem,
    send_sem,
    recv_sem,
):
    hours, patch_width = sky.shape
    blocks, depth, tile = view_w.shape
    sens_blocks = sens_w.shape[0]
    per = depth // tile
    patches = patch_width // tile
    me = lax.axis_index("surf")
    far = farthest_first(n)

    def out_to(step):
        if far is None:
            return lax.rem(me + step, n)
        to = me
        for bit in (1, 2, 4):
            if step & bit:
                to = to + bit * (1 - 2 * lax.rem(me // bit, 2))
        return to

    def in_from(step):
        return lax.rem(me + n - step, n) if far is None else out_to(step)

    barrier = pltpu.get_barrier_semaphore()

    def loop(low, high, body, group):
        count = high - low
        group = next(g for g in range(min(group, count), 0, -1) if count % g == 0)

        def go(i, carry):
            for u in range(group):
                body(low + i * group + u)
            return carry

        lax.fori_loop(0, count // group, go, 0)

    def each(turn, body):
        if far is None:
            loop(1, n, lambda step: body(turn(step)), 7)
        else:
            for step in range(1, n):
                body(turn(step))

    def each_far(body):
        if far is None:
            each(out_to, body)
        else:
            for step in far:
                body(out_to(step))

    def greet(peer):
        pl.semaphore_signal(
            barrier, inc=1, device_id={"surf": peer}, device_id_type=pl.DeviceIdType.MESH
        )

    each_far(greet)

    surf_parts = load_parts(blocks)
    sens_parts = load_parts(sens_blocks)

    def part(hbm, vmem, parts, i, first):
        size = vmem.shape[0] // parts
        span = pl.ds(i * size, size)
        return pltpu.make_async_copy(hbm.at[span], vmem.at[span], load_sem.at[first + i])

    surf_loads = [part(surf_hbm, surf_w, surf_parts, i, 0) for i in range(surf_parts)]
    view_load = part(view_hbm, view_w, 1, 0, surf_parts)
    sens_loads = [
        part(sens_hbm, sens_w, sens_parts, i, surf_parts + 1) for i in range(sens_parts)
    ]
    small = (
        (wanted_hbm.at[0], want_own),
        (sky_hbm, sky),
        (surf_patch_hbm, surf_patch),
        (surf_count_hbm, surf_count),
        (albedo_hbm, albedo),
        (view_peer_hbm, view_peer),
        (sens_patch_hbm, sens_patch),
        (sens_count_hbm, sens_count),
        (sens_surf_hbm, sens_surf),
        (sens_weight_hbm, weight),
    )
    small_loads = [
        pltpu.make_async_copy(src, dst, small_sem.at[i]) for i, (src, dst) in enumerate(small)
    ]
    early, late = small_loads[:5], small_loads[5:]
    for copy in (*early, *surf_loads, *late):
        copy.start()

    def remote(src, dst, kind, to, mine):
        return pltpu.make_async_remote_copy(
            src_ref=src,
            dst_ref=dst.at[mine],
            send_sem=send_sem.at[kind, to],
            recv_sem=recv_sem.at[kind, mine],
            device_id={"surf": to},
            device_id_type=pl.DeviceIdType.MESH,
        )

    early[0].wait()
    for e in range(n):
        want_rows[e] = jnp.full(want_rows.shape[1:], want_own[0, e], jnp.int32)
    want_v[me] = want_rows[me]
    pl.semaphore_wait(barrier, n - 1)
    each_far(lambda e: remote(want_rows.at[e], want_v, 0, e, me).start())

    early[1].wait()
    for j in range(patches):
        sky_tab[j] = sky[:, j * tile : (j + 1) * tile]
    sky_tab[patches] = jnp.zeros((hours, tile), BF16)

    def live(patch, count, k, b):
        return jnp.where(k < count[b], patch[k, b], patches)

    def direct_block(b):
        picks = [live(surf_patch, surf_count, k, b) for k in range(per)]
        value = wide_dot(sky_tab, picks, surf_w[b])
        direct[b] = value
        rad[b] = (value * albedo[b]).astype(BF16)

    def sens_block(b):
        picks = [live(sens_patch, sens_count, k, b) for k in range(per)]
        cols = pl.ds(pl.multiple_of(b * tile, tile), tile)
        sens_out[:, cols] = wide_dot(sky_tab, picks, sens_w[b])

    for copy in early[2:]:
        copy.wait()
    for i, copy in enumerate(surf_loads):
        copy.wait()
        size = blocks // surf_parts
        loop(i * size, (i + 1) * size, direct_block, 4)

    for copy in late:
        copy.wait()
    for copy in (*sens_loads[:2], view_load, *sens_loads[2:]):
        copy.start()
    place[...] = sens_surf[...] - me * (blocks * tile)

    def first_send(e):
        remote(want_rows.at[e], want_v, 0, me, e).wait_recv()
        send_a[e] = rad[jnp.max(want_v[e])]
        remote(send_a.at[e], slots_a, 1, e, me).start()

    if far is None:
        each(in_from, first_send)
    else:
        cuts = sorted({1, *(c for c in (3, 5) if c < n), n})
        for low, high in zip(cuts, cuts[1:]):
            peers = [in_from(step) for step in range(low, high)]
            for e in peers:
                remote(want_rows.at[e], want_v, 0, me, e).wait_recv()
            picks = [jnp.max(want_v[e]) for e in peers]
            for e, pick in zip(peers, picks):
                send_a[e] = rad[pick]
            for e in peers:
                remote(send_a.at[e], slots_a, 1, e, me).start()
    slots_a[me] = rad[jnp.max(want_v[me])]
    to_smem = pltpu.make_async_copy(want_v, want_s, want_sem.at[0])
    to_smem.start()

    half = sens_parts // 2
    rows = lax.broadcasted_iota(jnp.int32, (tile, 2 * tile), 0).astype(jnp.int16)
    ones = jnp.ones((tile, 2 * tile), BF16)
    zeros = jnp.zeros((tile, 2 * tile), BF16)

    def onehot_block(r):
        cols = pl.ds(pl.multiple_of(r * tile, tile), tile)
        index = place[:, cols]
        index = jnp.concatenate([index[0:1], index[1:2]], axis=1)
        index = jnp.broadcast_to(index, (tile, 2 * tile)).astype(jnp.int16)
        for s in range(blocks):
            hit = rows == index - jnp.int16(s * tile)
            onehot[r, s * tile : (s + 1) * tile, :] = jnp.where(hit, ones, zeros).astype(F8)

    def sens_part(i):
        sens_loads[i].wait()
        size = sens_blocks // sens_parts
        loop(i * size, (i + 1) * size, sens_block, 6)
        loop(i * size, (i + 1) * size, onehot_block, 1)

    for i in range(half):
        sens_part(i)

    view_load.wait()
    to_smem.wait()
    each(in_from, lambda e: remote(send_a.at[e], slots_a, 1, me, e).wait_recv())

    def bounced(slots, b):
        picks = [view_peer[k, b] for k in range(per)]
        return wide_dot(slots, picks, view_w[b])

    def asked(e):
        return want_s[e, 0, 0]

    def second_value(b):
        value = direct[b] + bounced(slots_a, b)
        return (value * albedo[b]).astype(BF16)

    def second_send(e):
        send_b[e] = second_value(asked(e))
        remote(send_b.at[e], slots_b, 2, e, me).start()

    if far is None:
        each_far(second_send)
    else:
        peers = [out_to(step) for step in far]
        cuts = sorted({0, *(c for c in (2, 4) if c < n - 1), n - 1})
        for low, high in zip(cuts, cuts[1:]):
            values = [second_value(asked(e)) for e in peers[low:high]]
            for e, value in zip(peers[low:high], values):
                send_b[e] = value
            for e in peers[low:high]:
                remote(send_b.at[e], slots_b, 2, e, me).start()
    slots_b[me] = second_value(asked(me))

    for i in range(half, sens_parts):
        sens_part(i)

    each(out_to, lambda e: remote(want_rows.at[e], want_v, 0, e, me).wait_send())
    each(out_to, lambda e: remote(send_a.at[e], slots_a, 1, e, me).wait_send())
    each(in_from, lambda e: remote(send_b.at[e], slots_b, 2, me, e).wait_recv())

    group = next(g for g in (16, 8, 4, 2, 1) if blocks % g == 0)

    def last_blocks(i, top):
        for u in range(group):
            b = i * group + u
            value = bounced(slots_b, b)
            cols = pl.ds(pl.multiple_of(b * tile, tile), tile)
            refl[:, cols] = value
            surf_out[:, cols] = direct[b] + value
            top = jnp.maximum(top, jnp.abs(value))
        return top

    most[...] = lax.fori_loop(0, blocks // group, last_blocks, jnp.full((hours, tile), 1e-30, F32))

    each(out_to, lambda e: remote(send_b.at[e], slots_b, 2, e, me).wait_send())


def load_parts(blocks):
    return 4 if blocks % 4 == 0 else 1


def local(
    sky_radiance,
    surf_coeff,
    surf_patch,
    surf_count,
    sens_coeff,
    sens_patch,
    sens_count,
    albedo,
    view_tile,
    view_peer,
    wanted,
    sens_surf,
    sens_weight,
):
    n = lax.axis_size("surf")
    hours, patch_width = sky_radiance.shape
    blocks, per, tile, _ = view_tile.shape
    sens_blocks = sens_coeff.shape[0]
    depth = per * tile
    patches = patch_width // tile

    hbm = pl.BlockSpec(memory_space=pltpu.HBM)
    vmem = pl.BlockSpec(memory_space=pltpu.VMEM)
    loads = load_parts(blocks) + 1 + load_parts(sens_blocks)
    made = pl.pallas_call(
        functools.partial(kernel, n),
        out_shape=(
            pltpu.VMEM((hours, blocks * tile), F32),
            pltpu.VMEM((hours, sens_blocks * tile), F32),
            pltpu.VMEM((hours, blocks * tile), F32),
            pltpu.VMEM((hours, tile), F32),
            pltpu.VMEM((sens_blocks, blocks * tile, 2 * tile), F8),
            pltpu.VMEM(sens_surf.shape, jnp.int32),
            pltpu.VMEM(sens_weight.shape, F32),
        ),
        in_specs=[hbm] * 13,
        out_specs=(vmem,) * 7,
        scratch_shapes=[
            pltpu.VMEM((hours, patch_width), BF16),
            pltpu.SMEM((per, blocks), jnp.int32),
            pltpu.SMEM((blocks,), jnp.int32),
            pltpu.SMEM((per, sens_blocks), jnp.int32),
            pltpu.SMEM((sens_blocks,), jnp.int32),
            pltpu.VMEM((blocks, 1, tile), F32),
            pltpu.SMEM((per, blocks), jnp.int32),
            pltpu.VMEM(sens_surf.shape, jnp.int32),
            pltpu.VMEM((patches + 1, hours, tile), BF16),
            pltpu.VMEM((blocks, depth, tile), BF16),
            pltpu.VMEM((sens_blocks, depth, tile), BF16),
            pltpu.VMEM((blocks, depth, tile), BF16),
            pltpu.VMEM((blocks, hours, tile), F32),
            pltpu.VMEM((blocks, hours, tile), BF16),
            pltpu.VMEM((n, hours, tile), BF16),
            pltpu.VMEM((n, hours, tile), BF16),
            pltpu.VMEM((n, hours, tile), BF16),
            pltpu.VMEM((n, hours, tile), BF16),
            pltpu.SMEM((1, n), jnp.int32),
            pltpu.VMEM((n, 1, tile), jnp.int32),
            pltpu.VMEM((n, 1, tile), jnp.int32),
            pltpu.SMEM((n, 1, tile), jnp.int32),
            pltpu.SemaphoreType.DMA((10,)),
            pltpu.SemaphoreType.DMA((loads,)),
            pltpu.SemaphoreType.DMA((2,)),
            pltpu.SemaphoreType.DMA((3, n)),
            pltpu.SemaphoreType.DMA((3, n)),
        ],
        compiler_params=pltpu.CompilerParams(
            collective_id=0, has_side_effects=True, vmem_limit_bytes=24 * 2**20
        ),
    )(
        *(
            pltpu.with_memory_space_constraint(a, pltpu.HBM)
            for a in (
                sky_radiance,
                surf_coeff.reshape(blocks, depth, tile),
                surf_patch.T,
                surf_count,
                sens_coeff.reshape(sens_blocks, depth, tile),
                sens_patch.T,
                sens_count,
                albedo.reshape(blocks, 1, tile),
                view_tile.reshape(blocks, depth, tile),
                view_peer.T,
                wanted.reshape(1, 1, n),
                sens_surf,
                sens_weight,
            )
        )
    )
    return sensors(*made)


def near(
    parts,
    surf,
    sens,
    refl,
    most,
    onehot,
    place,
    weight,
    surf_hbm,
    sens_hbm,
    out,
    pieces,
    sem,
):
    hours, width = refl.shape
    tile = onehot.shape[2] // 2
    stores = [pltpu.make_async_copy(surf, surf_hbm, sem.at[0])]
    stores[0].start()

    top = jnp.max(jnp.max(most[...], axis=0, keepdims=True), axis=1, keepdims=True)
    rest = refl[...] * (TOP / top)
    for i in range(3):
        piece = rest.astype(F8)
        pieces[i * hours : (i + 1) * hours, :] = piece
        rest = (rest - piece.astype(F32)) * STEP
    back = top * (1 / TOP)

    def by_matmul(cols, r):
        found = jnp.dot(pieces[...], onehot[r], preferred_element_type=F32)
        found = found[:hours] + (1 / STEP) * (
            found[hours : 2 * hours] + (1 / STEP) * found[2 * hours :]
        )
        gain = weight[:, cols] * back
        out[:, cols] = (
            sens[:, cols] + gain[0:1] * found[:, :tile] + gain[1:2] * found[:, tile:]
        )

    def by_gather(cols):
        block = place[:, cols] // tile
        lane = place[:, cols] - block * tile
        rows = 8
        shape = (rows, tile)
        for h in range(0, hours, rows):
            total = sens[h : h + rows, cols]
            for j in range(2):
                lanes = jnp.broadcast_to(lane[j : j + 1], shape)
                picked = jnp.broadcast_to(block[j : j + 1], shape)
                found = jnp.zeros(shape, F32)
                for s in range(width // tile):
                    part = refl[h : h + rows, s * tile : (s + 1) * tile]
                    part = jnp.take_along_axis(part, lanes, axis=1)
                    found = jnp.where(picked == s, part, found)
                total = total + jnp.broadcast_to(weight[j : j + 1, cols], shape) * found
            out[h : h + rows, cols] = total

    low = 0
    for i, high in enumerate(parts):
        for r in range(low, high):
            cols = pl.ds(r * tile, tile)
            if r == 0 or (r % 4 == 3 and r < parts[-1] - 4):
                by_gather(cols)
            else:
                by_matmul(cols, r)
        cols = pl.ds(low * tile, (high - low) * tile)
        copy = pltpu.make_async_copy(out.at[:, cols], sens_hbm.at[:, cols], sem.at[1 + i])
        copy.start()
        stores.append(copy)
        low = high
    for copy in stores:
        copy.wait()


def sensors(*arrays):
    surf, sens, refl = arrays[:3]
    hours, width = refl.shape
    count = arrays[4].shape[0]
    parts = [*range(6, count - 5, 6), count - 2, count] if count > 6 else [count]
    hbm = pl.BlockSpec(memory_space=pltpu.HBM)
    vmem = pl.BlockSpec(memory_space=pltpu.VMEM)
    return pl.pallas_call(
        functools.partial(near, parts),
        out_shape=(
            jax.ShapeDtypeStruct(surf.shape, F32),
            jax.ShapeDtypeStruct(sens.shape, F32),
        ),
        in_specs=[vmem] * 7,
        out_specs=(hbm, hbm),
        scratch_shapes=[
            pltpu.VMEM(sens.shape, F32),
            pltpu.VMEM((3 * hours, width), F8),
            pltpu.SemaphoreType.DMA((1 + len(parts),)),
        ],
        compiler_params=pltpu.CompilerParams(vmem_limit_bytes=8 * 2**20),
    )(*(pltpu.with_memory_space_constraint(a, pltpu.VMEM) for a in arrays))


def solution(mesh):
    in_specs = (
        P("hours", None),
        P("surf", None, None, None),
        P("surf", None),
        P("surf"),
        P("surf", None, None, None),
        P("surf", None),
        P("surf"),
        P("surf"),
        P("surf", None, None, None),
        P("surf", None),
        P("surf", None),
        P(None, "surf"),
        P(None, "surf"),
    )
    out_specs = (P("hours", "surf"), P("hours", "surf"))
    return jax.shard_map(local, mesh=mesh, in_specs=in_specs, out_specs=out_specs, check_vma=False)
```
